512 devices in a mesh: tm: 4 (over x), lat: 8 (over y), lon: 16 (over z, core).
Axes of the slice: x: 4, y: 8, z: 8, core: 2. Of those that a mesh axis runs over, the one named last changes fastest.
Arguments:
- start: float32 [4, 48, 128, 2048], P('tm', None, 'lat', 'lon'), may hold values from -6 to 6
- wet: int32 [128, 2048], P('lat', 'lon'), may hold values 0 or 1
- kappa: float32 [128, 2048], P('lat', 'lon'), may hold values from 0.06 to 0.24
- mixing: float32 [48, 48], replicated, may hold values from -0.12 to 0.12
Outputs:
- corrected_end: float32 [4, 48, 128, 2048], P('tm', None, 'lat', 'lon')
- next_start: float32 [4, 48, 128, 2048], P('tm', None, 'lat', 'lon')
The draws below stay inside these ranges and needn't reach their ends.
All inputs are finite; a program needn't handle non-finite values. No bound on the sum of `wet` on one device may be relied on, other than what follows from the above.
Results may differ from the reference program's by a relative error of at most 0.00018.
Values sent between devices are 32-bit elements; how exact they have to be, the bound alone decides.
No kernel may reach another device: no remote copies, remote signals or barrier semaphores. Data moves between devices by JAX's collectives and lax.ppermute only.
A program may use at most 64 MiB of HBM per device.

```python
import math
import jax
import jax.numpy as jnp
from jax import lax

K = 48
SLICES = 4
NY = 128
NX = 2048


def touch_ends(entries, own_key, low, top_value):
    longest = entries.shape.index(max(entries.shape))
    spots = []
    for shift in (0, 1):
        where = [jax.random.randint(jax.random.fold_in(own_key, axis), (), 0, length) for axis, length in enumerate(entries.shape)]
        where[longest] = (where[longest] + shift) % entries.shape[longest]
        spots.append(tuple(where))
    return entries.at[spots[0]].set(low).at[spots[1]].set(top_value)


def level_of(own_key, extent, pieces, least, top_value):
    loudness, own = 1.0, jax.random.fold_in(own_key, 6)
    for position, shards_of in pieces:
        steps = jnp.exp(jax.random.uniform(jax.random.fold_in(own, position), (shards_of,), jnp.float32, least / len(pieces), top_value / len(pieces)))
        loudness = loudness * jnp.repeat(steps, extent[position] // shards_of).reshape([-1 if axis == position else 1 for axis in range(len(extent))])
    return loudness


def normal_values(own_key, extent, deviation, limit, cuts=(), kind=jnp.bfloat16):
    loudness = level_of(own_key, extent, cuts, -0.22, 0.18) if cuts else 1.0
    drawn = jax.random.normal(own_key, extent, jnp.float32) * deviation * loudness
    return jnp.minimum(jnp.maximum(drawn, -limit), limit).astype(kind)


def setup_inputs(seed: int = 0) -> dict:
    key_of = jax.random.split(jax.random.key(seed), 5)
    start = normal_values(key_of[0], (SLICES, K, NY, NX), 1.0, 6.0, ((0, 4), (2, 8), (3, 16)), jnp.float32)
    wet = touch_ends((jax.random.randint(key_of[1], (NY, NX), 0, 4) < 3).astype(jnp.int32), jax.random.fold_in(key_of[1], 1), 0, 1)
    kappa = jnp.clip(jnp.exp(math.log(0.24) - 1.3862944 * jax.random.uniform(key_of[2], (NY, NX), jnp.float32) ** level_of(key_of[2], (NY, NX), ((0, 8), (1, 16)), -0.2, 0.2)), 0.06, 0.24)
    mixing = normal_values(key_of[3], (K, K), 0.02, 0.12, (), jnp.float32)
    return {"start": start, "wet": wet, "kappa": kappa, "mixing": mixing}


def pad_grid(field):
    widths = [(0, 0)] * (field.ndim - 2) + [(1, 1), (0, 0)]
    bordered_field = jnp.pad(field, widths)
    return jnp.concatenate([bordered_field[..., -1:], bordered_field, bordered_field[..., :1]], axis=-1)


def mesh_spacing(bordered_field, mask_bordered, diffusivity_bordered, vertical_matrix, laplacian_scale):
    middle_value = bordered_field[:, 1:-1, 1:-1]
    mask_mid = mask_bordered[1:-1, 1:-1]
    kap_mid = diffusivity_bordered[1:-1, 1:-1]
    parts = [(bordered_field[:, :-2, 1:-1], mask_bordered[:-2, 1:-1], diffusivity_bordered[:-2, 1:-1]),
             (bordered_field[:, 2:, 1:-1], mask_bordered[2:, 1:-1], diffusivity_bordered[2:, 1:-1]),
             (bordered_field[:, 1:-1, :-2], mask_bordered[1:-1, :-2], diffusivity_bordered[1:-1, :-2]),
             (bordered_field[:, 1:-1, 2:], mask_bordered[1:-1, 2:], diffusivity_bordered[1:-1, 2:])]
    lap = None
    for other, mask_other, kap_other in parts:
        term = 0.5 * (kap_mid + kap_other) * (mask_mid * mask_other) * (other - middle_value)
        lap = term if lap is None else lap + term
    depth_layers = middle_value.shape[0]
    vertical_term = jnp.dot(vertical_matrix, middle_value.reshape(depth_layers, -1), precision=lax.Precision.HIGHEST).reshape(middle_value.shape)
    return mask_mid * ((middle_value + laplacian_scale * lap) + vertical_term)


def block_sum(field):
    rows, cols = field.shape[-2], field.shape[-1]
    shaped = field.reshape(field.shape[:-2] + (rows // 2, 2, cols // 2, 2))
    return jnp.sum(shaped, axis=(-3, -1))


def prolong(field):
    return jnp.repeat(jnp.repeat(field, 2, axis=-2), 2, axis=-1)


def reference(start, wet, kappa, mixing):
    mask = wet.astype(jnp.float32)
    mask_bordered = pad_grid(mask)
    diffusivity_bordered = pad_grid(kappa)
    count = block_sum(mask)
    cmask_pad = pad_grid(jnp.minimum(count, 1.0))
    ckap_pad = pad_grid(block_sum(kappa) * 0.25)
    coarse_mix = 3.0 * mixing
    divisor = jnp.maximum(count, 1.0)

    def fine(field):
        for step in range(3):
            field = mesh_spacing(pad_grid(field), mask_bordered, diffusivity_bordered, mixing, 1.0)
        return field

    def restrict(field):
        return block_sum(mask * field) / divisor

    def coarse(field):
        return mesh_spacing(pad_grid(field), cmask_pad, ckap_pad, coarse_mix, 0.75)

    fine_ends, fine_coarse, jumps = [], [], []
    for slot in range(SLICES):
        fine_end = fine(start[slot])
        coarse_end = restrict(fine_end)
        fine_ends.append(fine_end)
        fine_coarse.append(coarse_end)
        if slot == 0:
            jumps.append(coarse_end)
        else:
            jumps.append(coarse_end - coarse(restrict(start[slot])))
    state = jumps[0]
    states = [state]
    for slot in range(1, SLICES):
        state = coarse(state) + jumps[slot]
        states.append(state)
    corrected = [fine_ends[n] + mask * prolong(states[n] - fine_coarse[n]) for n in range(SLICES)]
    corrected_end = jnp.stack(corrected)
    next_start = jnp.concatenate([start[:1], corrected_end[:-1]], axis=0)
    return corrected_end, next_start
```

```python
import functools

import jax
import jax.numpy as jnp
from jax import lax
from jax.experimental import pallas as pl
from jax.experimental.pallas import tpu as pltpu
from jax.sharding import PartitionSpec as P

K = 48
R = 16
C = 128
H = 9
E = R + 2 * H
W = 2 * C
G = K // 8
SLOT = 2 * H
BASE = R - H
NC = 16
VMEM = pl.BlockSpec(memory_space=pltpu.VMEM)
SMEM = pl.BlockSpec(memory_space=pltpu.SMEM)
PARAMS = pltpu.CompilerParams(vmem_limit_bytes=40 * 1024 * 1024)


def lanes(shape):
    return lax.broadcasted_iota(jnp.int32, shape, len(shape) - 1)


def shift(x, by):
    return pltpu.roll(x, by % x.shape[-1], x.ndim - 1)


def own_row(x_ref, r):
    return x_ref[pl.ds(r, K, stride=R), :]


def halo_kernel(x_ref, wet_ref, kap_ref, top_ref, bot_ref):
    mask = wet_ref[...].astype(jnp.float32)
    for i in range(H):
        top_ref[pl.ds(i * K, K), :] = own_row(x_ref, i) * mask[i : i + 1]
        j = R - H + i
        bot_ref[pl.ds(i * K, K), :] = own_row(x_ref, j) * mask[j : j + 1]
    for ref in (top_ref, bot_ref):
        ref[pl.ds(H * K, R), :] = mask
        ref[pl.ds(H * K + R, R), :] = kap_ref[...]


def pack_row(row):
    lane = lanes((8, C))
    out = shift(row[0:8], H)
    for g in range(1, G):
        out = jnp.where(lane < SLOT * g, out, shift(row[8 * g : 8 * g + 8], SLOT * g + H))
    return out


def unpack_row(packed):
    return jnp.concatenate([shift(packed, C - H - SLOT * g) for g in range(G)], axis=0)


def core_row(x_ref, mask, up_ref, down_ref, r):
    if r < H:
        return up_ref[pl.ds(r * K, K), :]
    if r < H + R:
        return own_row(x_ref, r - H) * mask[r - H : r - H + 1]
    return down_ref[pl.ds((r - H - R) * K, K), :]


def coef_rows(up_ref, own, down_ref, offset):
    at = pl.ds(H * K + offset, R)
    return jnp.concatenate([up_ref[at, :], own, down_ref[at, :]], axis=0)


def edge_kernel(x_ref, wet_ref, kap_ref, up_ref, down_ref, left_ref, right_ref):
    mask = wet_ref[...].astype(jnp.float32)
    rows = [core_row(x_ref, mask, up_ref, down_ref, r) for r in range(E)]
    rows.append(coef_rows(up_ref, mask, down_ref, 0))
    rows.append(coef_rows(up_ref, kap_ref[...], down_ref, R))
    half = len(rows) // 2
    low = lanes((8, C)) % SLOT < H
    for p in range(half):
        a, b = pack_row(rows[p]), pack_row(rows[p + half])
        left_ref[pl.ds(8 * p, 8), :] = jnp.where(low, a, shift(b, H))
        right_ref[pl.ds(8 * p, 8), :] = jnp.where(low, shift(a, -H), b)


def split(x):
    high = x.astype(jnp.bfloat16)
    return high, (x - high.astype(jnp.float32)).astype(jnp.bfloat16)


def level_matrix(mix):
    high, low = split(mix)
    return jnp.concatenate([high, high, low], axis=1)


def levels(matrix, u):
    high, low = split(u)
    return jnp.dot(
        matrix, jnp.concatenate([high, low, high], axis=0), preferred_element_type=jnp.float32
    )


def coefficients(m, k, up, down, scale, by, out_ref):
    total = None
    for i, move in enumerate((up, down, lambda a: shift(a, by), lambda a: shift(a, -by))):
        c = (0.5 * scale) * (k + move(k)) * (m * move(m))
        out_ref[i + 1] = c
        total = c if total is None else total + c
    out_ref[0] = m * (1.0 - total)


def stencil(coef_ref, row, by, u, north, south, matrix):
    c = [coef_ref[i, pl.ds(row, 1), :] for i in range(5)]
    near = c[0] * u + c[1] * north + c[2] * south
    side = c[3] * shift(u, by) + c[4] * shift(u, -by)
    return (near + side) + levels(matrix, u)


def pair_sum(x):
    even = lanes(x.shape) % 2 == 0
    return x + jnp.where(even, shift(x, -1), shift(x, 1))


def put_q(q_ref, out_ref, first, count):
    even = lanes((K, W)) % 2 == 0
    for p in range(count // 2):
        both = jnp.where(even, q_ref[first + 2 * p], q_ref[first + 2 * p + 1])
        out_ref[pl.ds(p * K, K), :] = both[:, :C]
        out_ref[pl.ds((count // 2) * K + 8 * p, 8), :] = pack_row(both[:, C:])


def take_q(in_ref, count, write):
    even = lanes((K, W)) % 2 == 0
    for p in range(count // 2):
        core = in_ref[pl.ds(p * K, K), :]
        side = unpack_row(in_ref[pl.ds((count // 2) * K + 8 * p, 8), :])
        both = jnp.concatenate([core, side], axis=1)
        write(2 * p, jnp.where(even, both, shift(both, 1)))
        write(2 * p + 1, jnp.where(even, shift(both, -1), both))


def fine_kernel(
    later_ref, x_ref, wet_ref, kap_ref, mix_ref, up_ref, down_ref, rl_ref, rr_ref,
    q3_ref, q2_ref, q1_ref, q0_ref, rest_ref, cc_ref,
    ua, ub, mk, cf, rs, qs,
):
    mask = wet_ref[...].astype(jnp.float32)
    half = (E + 2) // 2
    low = lanes((8, C)) % SLOT < H
    sides = []
    for p in range(half):
        a, b = rl_ref[pl.ds(8 * p, 8), :], rr_ref[pl.ds(8 * p, 8), :]
        sides.append((jnp.where(low, a, shift(b, H)), jnp.where(low, shift(a, -H), b)))
    sides = [s[0] for s in sides] + [s[1] for s in sides]
    for r in range(E):
        ua[r, :, :C] = core_row(x_ref, mask, up_ref, down_ref, r)
        ua[r, :, C:] = unpack_row(sides[r])
    mk[0] = coef_rows(up_ref, mask, down_ref, 0)
    mk[1] = unpack_row(sides[E])
    mk[2] = coef_rows(up_ref, kap_ref[...], down_ref, R)
    mk[3] = unpack_row(sides[E + 1])
    north = lambda a: pltpu.roll(a, 1, 0)
    south = lambda a: pltpu.roll(a, a.shape[0] - 1, 0)
    m = jnp.concatenate([mk[0], mk[1]], axis=1)
    k = jnp.concatenate([mk[2], mk[3]], axis=1)
    coefficients(m, k, north, south, 1.0, 1, cf)

    at, after = pl.ds(8, NC, stride=2), pl.ds(9, NC, stride=2)

    def blocks(i):
        return pair_sum(jnp.concatenate([mk[j, at] + mk[j, after] for j in (i, i + 1)], axis=1))

    count = blocks(0)
    inverse = 1.0 / jnp.maximum(count, 1.0)
    coefficients(jnp.minimum(count, 1.0), 0.25 * blocks(2), north, south, 0.75, 2, cc_ref.at[pl.ds(0, 5)])
    cc_ref[5] = inverse
    mix = mix_ref[...]
    fine_mix = level_matrix(mix)
    coarse_mix = level_matrix(3.0 * mix)

    def restrict(src, i):
        return pair_sum(src[1 + 2 * i] + src[2 + 2 * i]) * cc_ref[5, pl.ds(i, 1), :]

    @pl.loop(0, NC)
    def _(i):
        rs[i] = restrict(ua, i)

    def step(src, dst, margin):
        @pl.loop(margin, E - margin)
        def _(r):
            dst[r] = stencil(cf, r + BASE, 1, src[r], src[r - 1], src[r + 1], fine_mix)

    step(ua, ub, 1)
    step(ub, ua, 2)
    step(ua, ub, 3)
    later = later_ref[0]

    @pl.loop(1, NC - 1)
    def _(i):
        fc = restrict(ub, i)
        qs[i] = fc - later * stencil(cc_ref, i, 2, rs[i], rs[i - 1], rs[i + 1], coarse_mix)
        rs[i - 1] = fc

    for i in range(R // 2):
        fc = rs[3 + i, :, :C]
        q0_ref[i] = qs[4 + i, :, :C]
        for r in (2 * i, 2 * i + 1):
            rest_ref[pl.ds(r * K, K), :] = ub[H + r, :, :C] - mask[r : r + 1] * fc
    put_q(qs, q3_ref, 1, 14)
    put_q(qs, q2_ref, 2, 12)
    put_q(qs, q1_ref, 3, 10)


def sweep_kernel(
    wet_ref, mix_ref, cc_ref, q3_ref, q2_ref, q1_ref, q0_ref, rest_ref, out_ref, y_ref, a, b
):
    coarse_mix = level_matrix(3.0 * mix_ref[...])
    mask = wet_ref[...].astype(jnp.float32)

    def put(ref, first):
        def write(i, value):
            ref[first + i] = value

        return write

    def step(src, dst, first, count):
        @pl.loop(first, first + count)
        def _(i):
            dst[i] = dst[i] + stencil(cc_ref, i, 2, src[i], src[i - 1], src[i + 1], coarse_mix)

    take_q(q3_ref, 14, put(a, 1))
    take_q(q2_ref, 12, put(b, 2))
    step(a, b, 2, 12)
    take_q(q1_ref, 10, put(a, 3))
    step(b, a, 3, 10)
    for i in range(8):
        y_ref[i] = a[4 + i, :, :C]
        z = q0_ref[i] + stencil(cc_ref, 4 + i, 2, a[4 + i], a[3 + i], a[5 + i], coarse_mix)[:, :C]
        for r in (2 * i, 2 * i + 1):
            value = rest_ref[pl.ds(r * K, K), :] + mask[r : r + 1] * z
            out_ref[pl.ds(r, K, stride=R), :] = value


def last_kernel(later_ref, wet_ref, x_ref, y_ref, rest_ref, out_ref):
    mask = wet_ref[...].astype(jnp.float32)
    first = later_ref[0] == 0.0

    @pl.when(first)
    def _():
        out_ref[...] = x_ref[...]

    @pl.when(jnp.logical_not(first))
    def _():
        for r in range(R):
            value = rest_ref[pl.ds(r * K, K), :] + mask[r : r + 1] * y_ref[r // 2]
            out_ref[pl.ds(r, K, stride=R), :] = value


def f32(*shape):
    return jax.ShapeDtypeStruct(shape, jnp.float32)


def call(kernel, n_in, outs, scratch=(), smem=0):
    return pl.pallas_call(
        kernel,
        out_shape=outs,
        in_specs=[SMEM] * smem + [VMEM] * (n_in - smem),
        out_specs=jax.tree.map(lambda _: VMEM, outs),
        scratch_shapes=list(scratch),
        compiler_params=PARAMS,
    )


def moved(value, axis, by, wrap=False):
    n = lax.axis_size(axis)
    pairs = [(i, (i + by) % n) for i in range(n) if wrap or 0 <= i + by < n]
    return lax.ppermute(value, axis, pairs)


def body(start, wet, kappa, mixing):
    x = start.reshape(K * R, C)
    later = (lax.axis_index("tm") > 0).astype(jnp.float32).reshape(1)
    send = H * K + 2 * R
    top, bottom = call(halo_kernel, 3, (f32(send, C), f32(send, C)))(x, wet, kappa)
    down = moved(top, "lat", -1)
    up = moved(bottom, "lat", 1)
    side = (E + 2) * 4
    left, right = call(edge_kernel, 5, (f32(side, C), f32(side, C)))(x, wet, kappa, up, down)
    from_left = moved(left, "lon", 1, True)
    from_right = moved(right, "lon", -1, True)
    q3, q2, q1, q0, rest, cc = call(
        fine_kernel,
        9,
        (f32(49 * 8, C), f32(42 * 8, C), f32(35 * 8, C), f32(8, K, C), f32(R * K, C), f32(6, NC, W)),
        [
            pltpu.VMEM((E, K, W), jnp.float32),
            pltpu.VMEM((E, K, W), jnp.float32),
            pltpu.VMEM((4, 48, C), jnp.float32),
            pltpu.VMEM((5, 48, W), jnp.float32),
            pltpu.VMEM((NC, K, W), jnp.float32),
            pltpu.VMEM((NC, K, W), jnp.float32),
        ],
        smem=1,
    )(later, x, wet, kappa, mixing, up, down, from_left, from_right)
    q3, q2, q1 = moved(q3, "tm", 3), moved(q2, "tm", 2), moved(q1, "tm", 1)
    rest_before = moved(rest, "tm", 1)
    out, y = call(
        sweep_kernel,
        8,
        (f32(K * R, C), f32(8, K, C)),
        [pltpu.VMEM((NC, K, W), jnp.float32), pltpu.VMEM((NC, K, W), jnp.float32)],
    )(wet, mixing, cc, q3, q2, q1, q0, rest)
    following = call(last_kernel, 5, f32(K * R, C), smem=1)(later, wet, x, y, rest_before)
    return out.reshape(1, K, R, C), following.reshape(1, K, R, C)


def solution(mesh):
    in_specs = (P("tm", None, "lat", "lon"), P("lat", "lon"), P("lat", "lon"), P())
    out_specs = (P("tm", None, "lat", "lon"), P("tm", None, "lat", "lon"))
    return jax.shard_map(body, mesh=mesh, in_specs=in_specs, out_specs=out_specs, check_vma=False)
```

```python
import functools

import jax
import jax.numpy as jnp
from jax import lax
from jax.experimental import pallas as pl
from jax.experimental.pallas import tpu as pltpu
from jax.sharding import PartitionSpec as P

K = 48
R = 16
C = 128
H = 9
E = R + 2 * H
W = 2 * C
G = K // 8
SLOT = 2 * H
BASE = R - H
NC = 16
VMEM = pl.BlockSpec(memory_space=pltpu.VMEM)
SMEM = pl.BlockSpec(memory_space=pltpu.SMEM)
PARAMS = pltpu.CompilerParams(vmem_limit_bytes=40 * 1024 * 1024)


def lanes(shape):
    return lax.broadcasted_iota(jnp.int32, shape, len(shape) - 1)


def shift(x, by):
    return pltpu.roll(x, by % x.shape[-1], x.ndim - 1)


def halo_kernel(
    x_hbm, wet_hbm, kap_hbm, top_ref, bot_ref, core_ref, mk_ref, x_ref, wet_ref, kap_ref, sems
):
    copies = [
        pltpu.make_async_copy(src, dst, sems.at[i])
        for i, (src, dst) in enumerate(
            ((wet_hbm, wet_ref), (kap_hbm, kap_ref), (x_hbm, x_ref))
        )
    ]
    for copy in copies:
        copy.start()
    for copy in copies:
        copy.wait()
    mask = wet_ref[...].astype(jnp.float32)
    for r in range(R):
        row = x_ref[pl.ds(r, K, stride=R), :] * mask[r : r + 1]
        core_ref[pl.ds(r * K, K), :] = row
        if r < H:
            top_ref[pl.ds(r * K, K), :] = row
        if r >= R - H:
            bot_ref[pl.ds((r - R + H) * K, K), :] = row
    for ref, first in ((top_ref, H * K), (bot_ref, H * K), (mk_ref, 0)):
        ref[pl.ds(first, R), :] = mask
        ref[pl.ds(first + R, R), :] = kap_ref[...]


def pack_row(row):
    lane = lanes((8, C))
    out = shift(row[0:8], H)
    for g in range(1, G):
        out = jnp.where(lane < SLOT * g, out, shift(row[8 * g : 8 * g + 8], SLOT * g + H))
    return out


def unpack_row(packed):
    return jnp.concatenate([shift(packed, C - H - SLOT * g) for g in range(G)], axis=0)


def core_row(core_ref, up_ref, down_ref, r):
    for ref, first, count in ((up_ref, 0, H), (core_ref, H, R), (down_ref, H + R, H)):
        if first <= r < first + count:
            return ref[pl.ds((r - first) * K, K), :]


def coef_rows(up_ref, mk_ref, down_ref, i):
    at = pl.ds(H * K + i * R, R)
    return jnp.concatenate([up_ref[at, :], mk_ref[pl.ds(i * R, R), :], down_ref[at, :]], axis=0)


def edge_kernel(core_ref, mk_ref, up_ref, down_ref, left_ref, right_ref):
    rows = [core_row(core_ref, up_ref, down_ref, r) for r in range(E)]
    rows += [coef_rows(up_ref, mk_ref, down_ref, i) for i in range(2)]
    half = len(rows) // 2
    low = lanes((8, C)) % SLOT < H
    for p in range(half):
        a, b = pack_row(rows[p]), pack_row(rows[p + half])
        left_ref[pl.ds(8 * p, 8), :] = jnp.where(low, a, shift(b, H))
        right_ref[pl.ds(8 * p, 8), :] = jnp.where(low, shift(a, -H), b)


def split(x):
    high = x.astype(jnp.bfloat16)
    return high, (x - high.astype(jnp.float32)).astype(jnp.bfloat16)


def level_matrix(mix):
    high, low = split(mix)
    return jnp.concatenate([high, high, low], axis=1)


def levels(matrix, u):
    high, low = split(u)
    return jnp.dot(
        matrix, jnp.concatenate([high, low, high], axis=0), preferred_element_type=jnp.float32
    )


def coefficients(m, k, up, down, scale, by, out_ref):
    total = None
    for i, move in enumerate((up, down, lambda a: shift(a, by), lambda a: shift(a, -by))):
        c = (0.5 * scale) * (k + move(k)) * (m * move(m))
        out_ref[i + 1] = c
        total = c if total is None else total + c
    out_ref[0] = m * (1.0 - total)


def stencil(coef_ref, row, by, u, north, south, matrix):
    c = [coef_ref[i, pl.ds(row, 1), :] for i in range(5)]
    near = c[0] * u + c[1] * north + c[2] * south
    side = c[3] * shift(u, by) + c[4] * shift(u, -by)
    return (near + side) + levels(matrix, u)


def by_tile(fn, x):
    return jnp.concatenate([fn(x[:, :C]), fn(x[:, C:])], axis=1)


def pair_sum(x):
    return x + by_tile(lambda t: shift(t, -1), x)


def spread(x):
    return jnp.where(lanes(x.shape) % 2 == 0, x, shift(x, 1))


def put_q(q_ref, out_ref, first, count):
    even = lanes((K, W)) % 2 == 0
    for p in range(count // 2):
        odd = by_tile(lambda t: shift(t, 1), q_ref[first + 2 * p + 1])
        both = jnp.where(even, q_ref[first + 2 * p], odd)
        out_ref[pl.ds(p * K, K), :] = both[:, :C]
        out_ref[pl.ds((count // 2) * K + 8 * p, 8), :] = pack_row(both[:, C:])


def take_q(in_ref, count, write):
    for p in range(count // 2):
        core = in_ref[pl.ds(p * K, K), :]
        side = unpack_row(in_ref[pl.ds((count // 2) * K + 8 * p, 8), :])
        both = jnp.concatenate([core, side], axis=1)
        write(2 * p, both)
        write(2 * p + 1, by_tile(lambda t: shift(t, -1), both))


def fine_kernel(
    later_ref, core_ref, mk_ref, mix_ref, up_ref, down_ref, rl_ref, rr_ref,
    q3_ref, q2_ref, q1_ref, q0_ref, rest_ref, cc_ref,
    ua, ub, mk, cf, rs, qs,
):
    half = (E + 2) // 2
    low = lanes((8, C)) % SLOT < H
    sides = []
    for p in range(half):
        a, b = rl_ref[pl.ds(8 * p, 8), :], rr_ref[pl.ds(8 * p, 8), :]
        sides.append((jnp.where(low, a, shift(b, H)), jnp.where(low, shift(a, -H), b)))
    sides = [s[0] for s in sides] + [s[1] for s in sides]
    for r in range(E):
        ua[r, :, :C] = core_row(core_ref, up_ref, down_ref, r)
        ua[r, :, C:] = unpack_row(sides[r])
    mk[0] = coef_rows(up_ref, mk_ref, down_ref, 0)
    mk[1] = unpack_row(sides[E])
    mk[2] = coef_rows(up_ref, mk_ref, down_ref, 1)
    mk[3] = unpack_row(sides[E + 1])
    north = lambda a: pltpu.roll(a, 1, 0)
    south = lambda a: pltpu.roll(a, a.shape[0] - 1, 0)
    m = jnp.concatenate([mk[0], mk[1]], axis=1)
    k = jnp.concatenate([mk[2], mk[3]], axis=1)
    coefficients(m, k, north, south, 1.0, 1, cf)

    at, after = pl.ds(8, NC, stride=2), pl.ds(9, NC, stride=2)

    def blocks(i):
        return pair_sum(jnp.concatenate([mk[j, at] + mk[j, after] for j in (i, i + 1)], axis=1))

    count = blocks(0)
    inverse = 1.0 / jnp.maximum(count, 1.0)
    coefficients(jnp.minimum(count, 1.0), 0.25 * blocks(2), north, south, 0.75, 2, cc_ref.at[pl.ds(0, 5)])
    cc_ref[5] = inverse
    mix = mix_ref[...]
    fine_mix = level_matrix(mix)
    coarse_mix = level_matrix(3.0 * mix)

    def restrict(src, i):
        return pair_sum(src[1 + 2 * i] + src[2 + 2 * i]) * cc_ref[5, pl.ds(i, 1), :]

    @pl.loop(0, NC, unroll=8)
    def _(i):
        rs[i] = restrict(ua, i)

    def step(src, dst, margin):
        @pl.loop(margin, E - margin, unroll=8)
        def _(r):
            dst[r] = stencil(cf, r + BASE, 1, src[r], src[r - 1], src[r + 1], fine_mix)

    step(ua, ub, 1)
    step(ub, ua, 2)
    step(ua, ub, 3)
    later = later_ref[0]

    @pl.loop(1, NC - 1, unroll=7)
    def _(i):
        fc = restrict(ub, i)
        qs[i] = fc - later * stencil(cc_ref, i, 2, rs[i], rs[i - 1], rs[i + 1], coarse_mix)
        rs[i - 1] = fc

    for i in range(R // 2):
        fc = spread(rs[3 + i, :, :C])
        q0_ref[i] = qs[4 + i, :, :C]
        for r in (2 * i, 2 * i + 1):
            rest_ref[pl.ds(r * K, K), :] = ub[H + r, :, :C] - mk_ref[pl.ds(r, 1), :] * fc
    put_q(qs, q3_ref, 1, 14)
    put_q(qs, q2_ref, 2, 12)
    put_q(qs, q1_ref, 3, 10)


def sweep_kernel(
    mk_ref, mix_ref, cc_ref, q3_ref, q2_ref, q1_ref, q0_ref, rest_ref, out_ref, y_ref, a, b
):
    coarse_mix = level_matrix(3.0 * mix_ref[...])

    def put(ref, first):
        def write(i, value):
            ref[first + i] = value

        return write

    def step(src, dst, first, count):
        @pl.loop(first, first + count, unroll=count // 2)
        def _(i):
            dst[i] = dst[i] + stencil(cc_ref, i, 2, src[i], src[i - 1], src[i + 1], coarse_mix)

    take_q(q3_ref, 14, put(a, 1))
    take_q(q2_ref, 12, put(b, 2))
    step(a, b, 2, 12)
    take_q(q1_ref, 10, put(a, 3))
    step(b, a, 3, 10)
    for i in range(8):
        y_ref[i] = spread(a[4 + i, :, :C])
        z = q0_ref[i] + stencil(cc_ref, 4 + i, 2, a[4 + i], a[3 + i], a[5 + i], coarse_mix)[:, :C]
        z = spread(z)
        for r in (2 * i, 2 * i + 1):
            value = rest_ref[pl.ds(r * K, K), :] + mk_ref[pl.ds(r, 1), :] * z
            out_ref[pl.ds(r, K, stride=R), :] = value


def last_kernel(later_ref, mk_ref, x_ref, y_ref, rest_ref, out_ref):
    first = later_ref[0] == 0.0

    @pl.when(first)
    def _():
        out_ref[...] = x_ref[...]

    @pl.when(jnp.logical_not(first))
    def _():
        for r in range(R):
            value = rest_ref[pl.ds(r * K, K), :] + mk_ref[pl.ds(r, 1), :] * y_ref[r // 2]
            out_ref[pl.ds(r, K, stride=R), :] = value


def f32(*shape):
    return jax.ShapeDtypeStruct(shape, jnp.float32)


def call(kernel, n_in, outs, scratch=(), smem=0, spec=VMEM):
    return pl.pallas_call(
        kernel,
        out_shape=outs,
        in_specs=[SMEM] * smem + [spec] * (n_in - smem),
        out_specs=jax.tree.map(lambda _: VMEM, outs),
        scratch_shapes=list(scratch),
        compiler_params=PARAMS,
    )


def fine_call():
    return call(
        fine_kernel,
        8,
        (f32(49 * 8, C), f32(42 * 8, C), f32(35 * 8, C), f32(8, K, C), f32(R * K, C), f32(6, NC, W)),
        [
            pltpu.VMEM((E, K, W), jnp.float32),
            pltpu.VMEM((E, K, W), jnp.float32),
            pltpu.VMEM((4, 48, C), jnp.float32),
            pltpu.VMEM((5, 48, W), jnp.float32),
            pltpu.VMEM((NC, K, W), jnp.float32),
            pltpu.VMEM((NC, K, W), jnp.float32),
        ],
        smem=1,
    )


def moved(value, axis, by, wrap=False):
    n = lax.axis_size(axis)
    pairs = [(i, (i + by) % n) for i in range(n) if wrap or 0 <= i + by < n]
    return lax.ppermute(value, axis, pairs)


def body(start, wet, kappa, mixing):
    x = start.reshape(K * R, C)
    later = (lax.axis_index("tm") > 0).astype(jnp.float32).reshape(1)
    send = H * K + 2 * R
    top, bottom, core, mk = call(
        halo_kernel,
        3,
        (f32(send, C), f32(send, C), f32(R * K, C), f32(2 * R, C)),
        [
            pltpu.VMEM((K * R, C), jnp.float32),
            pltpu.VMEM((R, C), jnp.int32),
            pltpu.VMEM((R, C), jnp.float32),
            pltpu.SemaphoreType.DMA((3,)),
        ],
        spec=pl.BlockSpec(memory_space=pl.ANY),
    )(x, wet, kappa)
    down = moved(top, "lat", -1)
    up = moved(bottom, "lat", 1)
    side = (E + 2) * 4
    left, right = call(edge_kernel, 4, (f32(side, C), f32(side, C)))(core, mk, up, down)
    from_left = moved(left, "lon", 1, True)
    from_right = moved(right, "lon", -1, True)
    q3, q2, q1, q0, rest, cc = fine_call()(
        later, core, mk, mixing, up, down, from_left, from_right
    )
    q3, q2, q1 = moved(q3, "tm", 3), moved(q2, "tm", 2), moved(q1, "tm", 1)
    rest_before = moved(rest, "tm", 1)
    out, y = call(
        sweep_kernel,
        8,
        (f32(K * R, C), f32(8, K, C)),
        [pltpu.VMEM((NC, K, W), jnp.float32), pltpu.VMEM((NC, K, W), jnp.float32)],
    )(mk, mixing, cc, q3, q2, q1, q0, rest)
    following = call(last_kernel, 5, f32(K * R, C), smem=1)(later, mk, x, y, rest_before)
    return out.reshape(1, K, R, C), following.reshape(1, K, R, C)


def solution(mesh):
    in_specs = (P("tm", None, "lat", "lon"), P("lat", "lon"), P("lat", "lon"), P())
    out_specs = (P("tm", None, "lat", "lon"), P("tm", None, "lat", "lon"))
    return jax.shard_map(body, mesh=mesh, in_specs=in_specs, out_specs=out_specs, check_vma=False)
```

```python
import functools

import jax
import jax.numpy as jnp
from jax import lax
from jax.experimental import pallas as pl
from jax.experimental.pallas import tpu as pltpu
from jax.sharding import PartitionSpec as P

K = 48
R = 16
C = 128
H = 9
E = R + 2 * H
W = 2 * C
REACH = 3
G = K // 8
SLOT = 2 * H
BASE = R - H
NC = 16
VMEM = pl.BlockSpec(memory_space=pltpu.VMEM)
SMEM = pl.BlockSpec(memory_space=pltpu.SMEM)
PARAMS = pltpu.CompilerParams(vmem_limit_bytes=40 * 1024 * 1024)


def lanes(shape):
    return lax.broadcasted_iota(jnp.int32, shape, len(shape) - 1)


def shift(x, by):
    return pltpu.roll(x, by % x.shape[-1], x.ndim - 1)


def halo_kernel(x_ref, mk_ref, top_ref, bot_ref, core_ref):
    for r in range(R):
        row = x_ref[pl.ds(r, K, stride=R), :] * mk_ref[r : r + 1]
        core_ref[pl.ds(r * K, K), :] = row
        if r < H:
            top_ref[pl.ds(r * K, K), :] = row
        if r >= R - H:
            bot_ref[pl.ds((r - R + H) * K, K), :] = row
    for ref in (top_ref, bot_ref):
        ref[pl.ds(H * K, 2 * R), :] = mk_ref[...]


def pack_row(row):
    lane = lanes((8, C))
    out = shift(row[0:8], H)
    for g in range(1, G):
        out = jnp.where(lane < SLOT * g, out, shift(row[8 * g : 8 * g + 8], SLOT * g + H))
    return out


def unpack_row(packed):
    return jnp.concatenate([shift(packed, C - H - SLOT * g) for g in range(G)], axis=0)


def core_row(core_ref, up_ref, down_ref, r):
    for ref, first, count in ((up_ref, 0, H), (core_ref, H, R), (down_ref, H + R, H)):
        if first <= r < first + count:
            return ref[pl.ds((r - first) * K, K), :]


def coef_rows(up_ref, mk_ref, down_ref, i):
    at = pl.ds(H * K + i * R, R)
    return jnp.concatenate([up_ref[at, :], mk_ref[pl.ds(i * R, R), :], down_ref[at, :]], axis=0)


def edge_kernel(core_ref, mk_ref, up_ref, down_ref, left_ref, right_ref):
    rows = [core_row(core_ref, up_ref, down_ref, r) for r in range(E)]
    rows += [coef_rows(up_ref, mk_ref, down_ref, i) for i in range(2)]
    half = len(rows) // 2
    low = lanes((8, C)) % SLOT < H
    for p in range(half):
        a, b = pack_row(rows[p]), pack_row(rows[p + half])
        left_ref[pl.ds(8 * p, 8), :] = jnp.where(low, a, shift(b, H))
        right_ref[pl.ds(8 * p, 8), :] = jnp.where(low, shift(a, -H), b)


def split(x):
    high = x.astype(jnp.bfloat16)
    return high, (x - high.astype(jnp.float32)).astype(jnp.bfloat16)


def level_matrix(mix):
    high, low = split(mix)
    return jnp.concatenate([high, high, low], axis=1)


def levels(matrix, u):
    high, low = split(u)
    return jnp.dot(
        matrix, jnp.concatenate([high, low, high], axis=0), preferred_element_type=jnp.float32
    )


def coefficients(m, k, up, down, scale, by, out_ref):
    total = None
    for i, move in enumerate((up, down, lambda a: shift(a, by), lambda a: shift(a, -by))):
        c = (0.5 * scale) * (k + move(k)) * (m * move(m))
        out_ref[i + 1] = c
        total = c if total is None else total + c
    out_ref[0] = m * (1.0 - total)


def stencil(coef_ref, row, by, u, north, south, matrix):
    c = [coef_ref[i, pl.ds(row, 1), :] for i in range(5)]
    near = c[0] * u + c[1] * north + c[2] * south
    side = c[3] * shift(u, by) + c[4] * shift(u, -by)
    return (near + side) + levels(matrix, u)


def by_tile(fn, x):
    return jnp.concatenate([fn(x[:, :C]), fn(x[:, C:])], axis=1)


def pair_sum(x):
    return x + by_tile(lambda t: shift(t, -1), x)


def spread(x):
    return jnp.where(lanes(x.shape) % 2 == 0, x, shift(x, 1))


def put_q(q_ref, out_ref, first, count):
    even = lanes((K, W)) % 2 == 0
    for p in range(count // 2):
        odd = by_tile(lambda t: shift(t, 1), q_ref[first + 2 * p + 1])
        both = jnp.where(even, q_ref[first + 2 * p], odd)
        out_ref[pl.ds(p * K, K), :] = both[:, :C]
        out_ref[pl.ds((count // 2) * K + 8 * p, 8), :] = pack_row(both[:, C:])


def take_q(in_ref, count, write):
    for p in range(count // 2):
        core = in_ref[pl.ds(p * K, K), :]
        side = unpack_row(in_ref[pl.ds((count // 2) * K + 8 * p, 8), :])
        both = jnp.concatenate([core, side], axis=1)
        write(2 * p, both)
        write(2 * p + 1, by_tile(lambda t: shift(t, -1), both))


RING = [*range(REACH), *range(R - REACH, R)]
SIDE = range(2, 6)


def put_ring(src, out_ref):
    for i, r in enumerate(RING):
        out_ref[pl.ds(i * K, K), :] = src[H + r, :, :C]
    at = lanes((8, C)) % SLOT
    for i, r in enumerate(SIDE):
        a, b, c = (pack_row(src[H + r + d, :, :C]) for d in (0, 4, 8))
        both = jnp.where(at < 2 * REACH, shift(a, -2 * REACH), b)
        both = jnp.where(at < 4 * REACH, both, shift(c, 2 * REACH))
        out_ref[pl.ds(len(RING) * K + 8 * i, 8), :] = both


def take_ring(in_ref, inner_ref):
    rows = {r: in_ref[pl.ds(i * K, K), :] for i, r in enumerate(RING)}
    lane = lanes((K, C))
    inside = (lane >= REACH) & (lane < C - REACH)
    for i, r in enumerate(SIDE):
        packed = in_ref[pl.ds(len(RING) * K + 8 * i, 8), :]
        for d, by in ((0, 2 * REACH), (4, 0), (8, -2 * REACH)):
            if r + d not in rows:
                ends = unpack_row(shift(packed, by))
                rows[r + d] = jnp.where(inside, inner_ref[pl.ds((r + d) * K, K), :], ends)
    return [rows[r] for r in range(R)]


def inner_kernel(core_ref, mix_ref, cf_ref, out_ref, ua, ub):
    mix = level_matrix(mix_ref[...])
    for r in range(R):
        ua[r] = core_ref[pl.ds(r * K, K), :]
    for margin, src, dst in ((1, ua, ub), (2, ub, ua), (3, ua, None)):
        for r in range(margin, R - margin):
            value = stencil(cf_ref, r, 1, src[r], src[r - 1], src[r + 1], mix)
            if dst is None:
                out_ref[pl.ds(r * K, K), :] = value
            else:
                dst[r] = value
    for r in RING:
        out_ref[pl.ds(r * K, K), :] = jnp.zeros((K, C), jnp.float32)


def fine_kernel(
    later_ref, core_ref, mk_ref, mix_ref, up_ref, down_ref, rl_ref, rr_ref,
    q3_ref, q2_ref, q1_ref, q0_ref, ring_ref, rest_ref, cc_ref, fc_ref,
    ua, ub, mk, cf, rs, qs,
):
    half = (E + 2) // 2
    low = lanes((8, C)) % SLOT < H
    sides = []
    for p in range(half):
        a, b = rl_ref[pl.ds(8 * p, 8), :], rr_ref[pl.ds(8 * p, 8), :]
        sides.append((jnp.where(low, a, shift(b, H)), jnp.where(low, shift(a, -H), b)))
    sides = [s[0] for s in sides] + [s[1] for s in sides]
    for r in range(E):
        ua[r, :, :C] = core_row(core_ref, up_ref, down_ref, r)
        ua[r, :, C:] = unpack_row(sides[r])
    mk[0] = coef_rows(up_ref, mk_ref, down_ref, 0)
    mk[1] = unpack_row(sides[E])
    mk[2] = coef_rows(up_ref, mk_ref, down_ref, 1)
    mk[3] = unpack_row(sides[E + 1])
    north = lambda a: pltpu.roll(a, 1, 0)
    south = lambda a: pltpu.roll(a, a.shape[0] - 1, 0)
    m = jnp.concatenate([mk[0], mk[1]], axis=1)
    k = jnp.concatenate([mk[2], mk[3]], axis=1)
    coefficients(m, k, north, south, 1.0, 1, cf)

    at, after = pl.ds(8, NC, stride=2), pl.ds(9, NC, stride=2)

    def blocks(i):
        return pair_sum(jnp.concatenate([mk[j, at] + mk[j, after] for j in (i, i + 1)], axis=1))

    count = blocks(0)
    inverse = 1.0 / jnp.maximum(count, 1.0)
    coefficients(jnp.minimum(count, 1.0), 0.25 * blocks(2), north, south, 0.75, 2, cc_ref.at[pl.ds(0, 5)])
    cc_ref[5] = inverse
    mix = mix_ref[...]
    fine_mix = level_matrix(mix)
    coarse_mix = level_matrix(3.0 * mix)

    def restrict(src, i):
        return pair_sum(src[1 + 2 * i] + src[2 + 2 * i]) * cc_ref[5, pl.ds(i, 1), :]

    @pl.loop(0, NC, unroll=8)
    def _(i):
        rs[i] = restrict(ua, i)

    def step(src, dst, margin):
        @pl.loop(margin, E - margin, unroll=8)
        def _(r):
            dst[r] = stencil(cf, r + BASE, 1, src[r], src[r - 1], src[r + 1], fine_mix)

    step(ua, ub, 1)
    step(ub, ua, 2)
    step(ua, ub, 3)
    later = later_ref[0]

    @pl.loop(1, NC - 1, unroll=7)
    def _(i):
        fc = restrict(ub, i)
        qs[i] = fc - later * stencil(cc_ref, i, 2, rs[i], rs[i - 1], rs[i + 1], coarse_mix)
        rs[i - 1] = fc

    for i in range(R // 2):
        fc = spread(rs[3 + i, :, :C])
        q0_ref[i] = qs[4 + i, :, :C]
        for r in (2 * i, 2 * i + 1):
            rest_ref[pl.ds(r * K, K), :] = ub[H + r, :, :C] - mk_ref[pl.ds(r, 1), :] * fc
    put_ring(ub, ring_ref)
    for i in range(5):
        fc_ref[i] = cf[i, pl.ds(R, R), :C]
    put_q(qs, q3_ref, 1, 14)
    put_q(qs, q2_ref, 2, 12)
    put_q(qs, q1_ref, 3, 10)


def sweep_kernel(
    mk_ref, mix_ref, cc_ref, q3_ref, q2_ref, q1_ref, q0_ref, rest_ref, out_ref, y_ref, a, b
):
    coarse_mix = level_matrix(3.0 * mix_ref[...])

    def put(ref, first):
        def write(i, value):
            ref[first + i] = value

        return write

    def step(src, dst, first, count):
        @pl.loop(first, first + count, unroll=count // 2)
        def _(i):
            dst[i] = dst[i] + stencil(cc_ref, i, 2, src[i], src[i - 1], src[i + 1], coarse_mix)

    take_q(q3_ref, 14, put(a, 1))
    take_q(q2_ref, 12, put(b, 2))
    step(a, b, 2, 12)
    take_q(q1_ref, 10, put(a, 3))
    step(b, a, 3, 10)
    for i in range(8):
        y_ref[i] = a[4 + i, :, :C]
        z = q0_ref[i] + stencil(cc_ref, 4 + i, 2, a[4 + i], a[3 + i], a[5 + i], coarse_mix)[:, :C]
        z = spread(z)
        for r in (2 * i, 2 * i + 1):
            value = rest_ref[pl.ds(r * K, K), :] + mk_ref[pl.ds(r, 1), :] * z
            out_ref[pl.ds(r, K, stride=R), :] = value


def last_kernel(later_ref, mk_ref, cc_ref, x_ref, y_ref, ring_ref, inner_ref, out_ref):
    first = later_ref[0] == 0.0

    @pl.when(first)
    def _():
        out_ref[...] = x_ref[...]

    @pl.when(jnp.logical_not(first))
    def _():
        rows = take_ring(ring_ref, inner_ref)
        for i in range(R // 2):
            above, below = rows[2 * i], rows[2 * i + 1]
            total = above + below
            fc = (total + shift(total, -1)) * cc_ref[5, 4 + i : 5 + i, :C]
            jump = spread(y_ref[i] - fc)
            for r, value in ((2 * i, above), (2 * i + 1, below)):
                out_ref[pl.ds(r, K, stride=R), :] = value + mk_ref[pl.ds(r, 1), :] * jump


def f32(*shape):
    return jax.ShapeDtypeStruct(shape, jnp.float32)


def call(kernel, n_in, outs, scratch=(), smem=0):
    return pl.pallas_call(
        kernel,
        out_shape=outs,
        in_specs=[SMEM] * smem + [VMEM] * (n_in - smem),
        out_specs=jax.tree.map(lambda _: VMEM, outs),
        scratch_shapes=list(scratch),
        compiler_params=PARAMS,
    )


def fine_call():
    return call(
        fine_kernel,
        8,
        (f32(49 * 8, C), f32(42 * 8, C), f32(35 * 8, C), f32(8, K, C), f32(40 * 8, C), f32(R * K, C), f32(6, NC, W), f32(5, R, C)),
        [
            pltpu.VMEM((E, K, W), jnp.float32),
            pltpu.VMEM((E, K, W), jnp.float32),
            pltpu.VMEM((4, 48, C), jnp.float32),
            pltpu.VMEM((5, 48, W), jnp.float32),
            pltpu.VMEM((NC, K, W), jnp.float32),
            pltpu.VMEM((NC, K, W), jnp.float32),
        ],
        smem=1,
    )


def moved(value, axis, by, wrap=False):
    n = lax.axis_size(axis)
    pairs = [(i, (i + by) % n) for i in range(n) if wrap or 0 <= i + by < n]
    return lax.ppermute(value, axis, pairs)


def body(start, wet, kappa, mixing):
    x = start.reshape(K * R, C)
    later = (lax.axis_index("tm") > 0).astype(jnp.float32).reshape(1)
    send = H * K + 2 * R
    mk = jnp.concatenate([wet.astype(jnp.float32), kappa], axis=0)
    top, bottom, core = call(halo_kernel, 2, (f32(send, C), f32(send, C), f32(R * K, C)))(x, mk)
    down = moved(top, "lat", -1)
    up = moved(bottom, "lat", 1)
    side = (E + 2) * 4
    left, right = call(edge_kernel, 4, (f32(side, C), f32(side, C)))(core, mk, up, down)
    from_left = moved(left, "lon", 1, True)
    from_right = moved(right, "lon", -1, True)
    before = moved(core, "tm", 1)
    q3, q2, q1, q0, ring, rest, cc, cf = fine_call()(
        later, core, mk, mixing, up, down, from_left, from_right
    )
    q3, q2, q1 = moved(q3, "tm", 3), moved(q2, "tm", 2), moved(q1, "tm", 1)
    ring_before = moved(ring, "tm", 1)
    inner = call(
        inner_kernel,
        3,
        f32(R * K, C),
        [pltpu.VMEM((R, K, C), jnp.float32), pltpu.VMEM((R, K, C), jnp.float32)],
    )(before, mixing, cf)
    out, y = call(
        sweep_kernel,
        8,
        (f32(K * R, C), f32(8, K, C)),
        [pltpu.VMEM((NC, K, W), jnp.float32), pltpu.VMEM((NC, K, W), jnp.float32)],
    )(mk, mixing, cc, q3, q2, q1, q0, rest)
    following = call(last_kernel, 7, f32(K * R, C), smem=1)(
        later, mk, cc, x, y, ring_before, inner
    )
    return out.reshape(1, K, R, C), following.reshape(1, K, R, C)


def solution(mesh):
    in_specs = (P("tm", None, "lat", "lon"), P("lat", "lon"), P("lat", "lon"), P())
    out_specs = (P("tm", None, "lat", "lon"), P("tm", None, "lat", "lon"))
    return jax.shard_map(body, mesh=mesh, in_specs=in_specs, out_specs=out_specs, check_vma=False)
```

```python
import jax
import jax.numpy as jnp
from jax import lax
from jax.experimental import pallas as pl
from jax.experimental.pallas import tpu as pltpu
from jax.sharding import PartitionSpec as P

K = 48
R = 16
C = 128
H = 9
E = R + 2 * H
W = 2 * C
G = K // 8
SLOT = 2 * H
BASE = R - H
NC = 16
REACH = 3
RING = [*range(REACH), *range(R - REACH, R)]
SIDE = range(2, 6)
Q3, Q2, Q1, RG = 49 * 8, 42 * 8, 35 * 8, 40 * 8
LAT = H * K + 8 * H + 2 * R + 8
VMEM = pl.BlockSpec(memory_space=pltpu.VMEM)
SMEM = pl.BlockSpec(memory_space=pltpu.SMEM)
ANY = pl.BlockSpec(memory_space=pl.ANY)


def lanes(shape):
    return lax.broadcasted_iota(jnp.int32, shape, len(shape) - 1)


def shift(x, by):
    return pltpu.roll(x, by % x.shape[-1], x.ndim - 1)


def by_tile(fn, x):
    return jnp.concatenate([fn(x[:, :C]), fn(x[:, C:])], axis=1)


def pair_sum(x):
    return x + by_tile(lambda t: shift(t, -1), x)


def spread(x):
    return jnp.where(lanes(x.shape) % 2 == 0, x, shift(x, 1))


def pack_row(row):
    lane = lanes((8, C))
    out = shift(row[0:8], H)
    for g in range(1, G):
        out = jnp.where(lane < SLOT * g, out, shift(row[8 * g : 8 * g + 8], SLOT * g + H))
    return out


def unpack_row(packed):
    return jnp.concatenate([shift(packed, C - H - SLOT * g) for g in range(G)], axis=0)


def edge_kernel(x_ref, mk_ref, left_ref, right_ref, core_ref):
    rows = []
    for r in range(R):
        row = x_ref[pl.ds(r, K, stride=R), :] * mk_ref[r : r + 1]
        core_ref[pl.ds(r * K, K), :] = row
        rows.append(pack_row(row))
    coefs = pack_row(jnp.concatenate([mk_ref[...], jnp.zeros((R, C), jnp.float32)], axis=0))
    rows += [coefs, coefs]
    half = len(rows) // 2
    low = lanes((8, C)) % SLOT < H
    for p in range(half):
        a, b = rows[p], rows[p + half]
        left_ref[pl.ds(8 * p, 8), :] = jnp.where(low, a, shift(b, H))
        right_ref[pl.ds(8 * p, 8), :] = jnp.where(low, shift(a, -H), b)


def halo_kernel(core_in, mk_ref, rl_ref, rr_ref, core_ref, top_ref, bot_ref, side_ref):
    half = (R + 2) // 2
    low = lanes((8, C)) % SLOT < H
    for p in range(half):
        a, b = rl_ref[pl.ds(8 * p, 8), :], rr_ref[pl.ds(8 * p, 8), :]
        side_ref[pl.ds(8 * p, 8), :] = jnp.where(low, a, shift(b, H))
        side_ref[pl.ds(8 * (p + half), 8), :] = jnp.where(low, shift(a, -H), b)
    for ref, first in ((top_ref, 0), (bot_ref, R - H)):
        ref[pl.ds(0, H * K), :] = core_in[pl.ds(first * K, H * K), :]
        ref[pl.ds(H * K, 8 * H), :] = side_ref[pl.ds(8 * first, 8 * H), :]
        ref[pl.ds(H * K + 8 * H, 2 * R), :] = mk_ref[...]
        ref[pl.ds(H * K + 8 * H + 2 * R, 8), :] = side_ref[pl.ds(8 * R, 8), :]


def split(x):
    high = x.astype(jnp.bfloat16)
    return high, (x - high.astype(jnp.float32)).astype(jnp.bfloat16)


def level_matrix(mix):
    high, low = split(mix)
    return jnp.concatenate([high, high, low], axis=1)


def levels(matrix, u):
    high, low = split(u)
    return jnp.dot(
        matrix, jnp.concatenate([high, low, high], axis=0), preferred_element_type=jnp.float32
    )


def coefficients(m, k, scale, by, out_ref):
    moves = (
        lambda a: pltpu.roll(a, 1, 0),
        lambda a: pltpu.roll(a, a.shape[0] - 1, 0),
        lambda a: shift(a, by),
        lambda a: shift(a, -by),
    )
    total = None
    for i, move in enumerate(moves):
        c = (0.5 * scale) * (k + move(k)) * (m * move(m))
        out_ref[i + 1] = c
        total = c if total is None else total + c
    out_ref[0] = m * (1.0 - total)


def fine_coarse_coefficients(mk, first, count, cf_ref, cc_ref):
    wide = lambda i: jnp.concatenate([mk[i], mk[i + 1]], axis=1)
    coefficients(wide(0), wide(2), 1.0, 1, cf_ref)
    at, after = pl.ds(first, count, stride=2), pl.ds(first + 1, count, stride=2)

    def blocks(i):
        return pair_sum(jnp.concatenate([mk[j, at] + mk[j, after] for j in (i, i + 1)], axis=1))

    wet = blocks(0)
    coefficients(
        jnp.minimum(wet, 1.0), 0.25 * blocks(2), 0.75, 2, cc_ref.at[pl.ds(0, 5)]
    )
    cc_ref[5] = 1.0 / jnp.maximum(wet, 1.0)


def stencil(coef_ref, row, by, u, north, south, matrix):
    c = [coef_ref[i, pl.ds(row, 1), :] for i in range(5)]
    near = c[0] * u + c[1] * north + c[2] * south
    side = c[3] * shift(u, by) + c[4] * shift(u, -by)
    return (near + side) + levels(matrix, u)


def step_row(src, r, coef_ref, row, by, matrix):
    return stencil(coef_ref, row, by, src[r], src[r - 1], src[r + 1], matrix)


def restrict(src, i, cc_ref, row):
    return pair_sum(src[1 + 2 * i] + src[2 + 2 * i]) * cc_ref[5, pl.ds(row, 1), :]


def own_kernel(
    later_ref, core_ref, side_ref, mk_ref, mix_ref, u0, u1, u2, u3, rs, gs, qs, mk, cf, cc
):
    for r in range(R):
        u0[H + r, :, :C] = core_ref[pl.ds(r * K, K), :]
        u0[H + r, :, C:] = unpack_row(side_ref[pl.ds(8 * r, 8), :])
    coefs = unpack_row(side_ref[pl.ds(8 * R, 8), :])
    for i in range(2):
        mk[2 * i] = mk_ref[pl.ds(i * R, R), :]
        mk[2 * i + 1] = coefs[i * R : i * R + R]
    fine_coarse_coefficients(mk, 0, R // 2, cf, cc)
    mix = mix_ref[...]
    fine_mix = level_matrix(mix)
    coarse_mix = level_matrix(3.0 * mix)
    for margin, src, dst in ((1, u0, u1), (2, u1, u2), (3, u2, u3)):

        @pl.loop(margin, R - margin, unroll=R - 2 * margin)
        def _(r):
            dst[H + r] = step_row(src, H + r, cf, r, 1, fine_mix)

    for i in range(4, 12):
        rs[i] = restrict(u0, i, cc, i - 4)
    for i in range(5, 11):
        gs[i] = step_row(rs, i, cc, i - 4, 2, coarse_mix)
    for i in range(6, 10):
        qs[i] = restrict(u3, i, cc, i - 4) - later_ref[0] * gs[i]


def put_q(q_ref, out_ref, first, count):
    even = lanes((K, W)) % 2 == 0
    for p in range(count // 2):
        odd = by_tile(lambda t: shift(t, 1), q_ref[first + 2 * p + 1])
        both = jnp.where(even, q_ref[first + 2 * p], odd)
        out_ref[pl.ds(p * K, K), :] = both[:, :C]
        out_ref[pl.ds((count // 2) * K + 8 * p, 8), :] = pack_row(both[:, C:])


def take_q(in_ref, count, write):
    for p in range(count // 2):
        core = in_ref[pl.ds(p * K, K), :]
        side = unpack_row(in_ref[pl.ds((count // 2) * K + 8 * p, 8), :])
        both = jnp.concatenate([core, side], axis=1)
        write(2 * p, both)
        write(2 * p + 1, by_tile(lambda t: shift(t, -1), both))


def put_ring(src, out_ref):
    for i, r in enumerate(RING):
        out_ref[pl.ds(Q1 + i * K, K), :] = src[H + r, :, :C]
    at = lanes((8, C)) % SLOT
    for i, r in enumerate(SIDE):
        a, b, c = (pack_row(src[H + r + d, :, :C]) for d in (0, 4, 8))
        both = jnp.where(at < 2 * REACH, shift(a, -2 * REACH), b)
        both = jnp.where(at < 4 * REACH, both, shift(c, 2 * REACH))
        out_ref[pl.ds(Q1 + len(RING) * K + 8 * i, 8), :] = both


def take_ring(in_ref, inner_ref):
    rows = {r: in_ref[pl.ds(Q1 + i * K, K), :] for i, r in enumerate(RING)}
    lane = lanes((K, C))
    inside = (lane >= REACH) & (lane < C - REACH)
    for i, r in enumerate(SIDE):
        packed = in_ref[pl.ds(Q1 + len(RING) * K + 8 * i, 8), :]
        for d, by in ((0, 2 * REACH), (4, 0), (8, -2 * REACH)):
            if r + d not in rows:
                ends = unpack_row(shift(packed, by))
                rows[r + d] = jnp.where(inside, inner_ref[pl.ds((r + d) * K, K), :], ends)
    return [rows[r] for r in range(R)]


def outer_kernel(
    later_ref, mk_ref, side_ref, mix_ref, up_ref, down_ref,
    _u0, _u1, _u2, _u3, _rs, _gs, _qs,
    u0, u1, u2, u3, rs, gs, qs, q3_ref, q2_ref, q1_ref, cc, core_cf, mk, cf,
):
    for ref, first in ((up_ref, 0), (down_ref, H + R)):
        for i in range(H):
            u0[first + i, :, :C] = ref[pl.ds(i * K, K), :]
            u0[first + i, :, C:] = unpack_row(ref[pl.ds(H * K + 8 * i, 8), :])
    for j, (ref, at, side, side_at) in enumerate(
        (
            (up_ref, H * K + 8 * H, up_ref, H * K + 8 * H + 2 * R),
            (mk_ref, 0, side_ref, 8 * R),
            (down_ref, H * K + 8 * H, down_ref, H * K + 8 * H + 2 * R),
        )
    ):
        coefs = unpack_row(side[pl.ds(side_at, 8), :])
        for i in range(2):
            mk[2 * i, pl.ds(j * R, R), :] = ref[pl.ds(at + i * R, R), :]
            mk[2 * i + 1, pl.ds(j * R, R), :] = coefs[i * R : i * R + R]
    fine_coarse_coefficients(mk, R - 8, NC, cf, cc)
    mix = mix_ref[...]
    fine_mix = level_matrix(mix)
    coarse_mix = level_matrix(3.0 * mix)
    for margin, src, dst in ((1, u0, u1), (2, u1, u2), (3, u2, u3)):

        @pl.loop(0, H, unroll=H)
        def _(i):
            for r in (margin + i, E - 1 - margin - i):
                dst[r] = step_row(src, r, cf, r + BASE, 1, fine_mix)

    for i in (0, 1, 2, 3, 12, 13, 14, 15):
        rs[i] = restrict(u0, i, cc, i)
    for i in (1, 2, 3, 4, 11, 12, 13, 14):
        gs[i] = step_row(rs, i, cc, i, 2, coarse_mix)
    for i in (1, 2, 3, 4, 5, 10, 11, 12, 13, 14):
        qs[i] = restrict(u3, i, cc, i) - later_ref[0] * gs[i]
    put_q(qs, q3_ref, 1, 14)
    put_q(qs, q2_ref, 2, 12)
    put_q(qs, q1_ref, 3, 10)
    put_ring(u3, q1_ref)
    for i in range(5):
        core_cf[i] = cf[i, pl.ds(R, R), :C]


def before_kernel(core_ref, mix_ref, cf_ref, u3, cc_ref, mk_ref, inner_ref, rest_ref, ua, ub):
    mix = level_matrix(mix_ref[...])
    for r in range(R):
        ua[r] = core_ref[pl.ds(r * K, K), :]
    for margin, src, dst in ((1, ua, ub), (2, ub, ua), (3, ua, None)):
        for r in range(margin, R - margin):
            value = step_row(src, r, cf_ref, r, 1, mix)
            if dst is None:
                inner_ref[pl.ds(r * K, K), :] = value
            else:
                dst[r] = value
    for r in RING:
        inner_ref[pl.ds(r * K, K), :] = jnp.zeros((K, C), jnp.float32)
    for i in range(R // 2):
        pair = [u3[H + r, :, :C] for r in (2 * i, 2 * i + 1)]
        fc = spread(block_mean(pair, cc_ref, i))
        for r, value in zip((2 * i, 2 * i + 1), pair):
            rest_ref[pl.ds(r * K, K), :] = value - mk_ref[pl.ds(r, 1), :] * fc


def block_mean(pair, cc_ref, i):
    total = pair[0] + pair[1]
    return (total + shift(total, -1)) * cc_ref[5, 4 + i : 5 + i, :C]


def sweep_kernel(mix_ref, cc_ref, q3_ref, q2_ref, b, a):
    coarse_mix = level_matrix(3.0 * mix_ref[...])
    take_q(q3_ref, 14, lambda i, value: a.__setitem__(1 + i, value))
    take_q(q2_ref, 12, lambda i, value: b.__setitem__(2 + i, value))
    for i in range(2, 14):
        b[i] = b[i] + step_row(a, i, cc_ref, i, 2, coarse_mix)


def last_kernel(
    later_ref, mk_ref, mix_ref, cc_ref, x_ref, b, q1_ref, qs, rest_ref, inner_ref,
    out_hbm, next_hbm, a, out_ref, next_ref, sems,
):
    coarse_mix = level_matrix(3.0 * mix_ref[...])
    take_q(q1_ref, 10, lambda i, value: a.__setitem__(3 + i, value))
    for i in range(3, 13):
        a[i] = a[i] + step_row(b, i, cc_ref, i, 2, coarse_mix)
    first = later_ref[0] == 0.0

    @pl.when(first)
    def _():
        next_ref[...] = x_ref[...]

    @pl.when(jnp.logical_not(first))
    def _():
        rows = take_ring(q1_ref, inner_ref)
        for i in range(R // 2):
            pair = rows[2 * i], rows[2 * i + 1]
            jump = spread(a[4 + i, :, :C] - block_mean(pair, cc_ref, i))
            for r, value in zip((2 * i, 2 * i + 1), pair):
                next_ref[pl.ds(r, K, stride=R), :] = value + mk_ref[pl.ds(r, 1), :] * jump

    next_copy = pltpu.make_async_copy(next_ref, next_hbm, sems.at[0])
    next_copy.start()
    for i in range(R // 2):
        z = qs[4 + i] + step_row(a, 4 + i, cc_ref, 4 + i, 2, coarse_mix)
        z = spread(z[:, :C])
        for r in (2 * i, 2 * i + 1):
            value = rest_ref[pl.ds(r * K, K), :] + mk_ref[pl.ds(r, 1), :] * z
            out_ref[pl.ds(r, K, stride=R), :] = value
    out_copy = pltpu.make_async_copy(out_ref, out_hbm, sems.at[1])
    out_copy.start()
    next_copy.wait()
    out_copy.wait()


def f32(*shape):
    return jax.ShapeDtypeStruct(shape, jnp.float32)


def scratch(*shape):
    return pltpu.VMEM(shape, jnp.float32)


def call(kernel, n_in, outs, scratches=(), smem=0, aliases=None, out_spec=VMEM):
    return pl.pallas_call(
        kernel,
        out_shape=outs,
        in_specs=[SMEM] * smem + [VMEM] * (n_in - smem),
        out_specs=jax.tree.map(lambda _: out_spec, outs),
        scratch_shapes=list(scratches),
        input_output_aliases=aliases or {},
        compiler_params=pltpu.CompilerParams(vmem_limit_bytes=40 * 1024 * 1024),
    )


def moved(value, axis, by, wrap=False):
    n = lax.axis_size(axis)
    pairs = [(i, (i + by) % n) for i in range(n) if wrap or 0 <= i + by < n]
    return lax.ppermute(value, axis, pairs)


def body(start, wet, kappa, mixing):
    x = start.reshape(K * R, C)
    later = (lax.axis_index("tm") > 0).astype(jnp.float32).reshape(1)
    mk = jnp.concatenate([wet.astype(jnp.float32), kappa], axis=0)
    lon = (R + 2) * 4
    left, right, core = call(edge_kernel, 2, (f32(lon, C), f32(lon, C), f32(R * K, C)))(x, mk)
    from_left = moved(left, "lon", 1, True)
    from_right = moved(right, "lon", -1, True)
    core, top, bottom, side = call(
        halo_kernel,
        4,
        (f32(R * K, C), f32(LAT, C), f32(LAT, C), f32(8 * (R + 2), C)),
        aliases={0: 0},
    )(core, mk, from_left, from_right)
    down = moved(top, "lat", -1)
    up = moved(bottom, "lat", 1)
    before = moved(core, "tm", 1)
    fine, coarse = f32(E, K, W), f32(NC, K, W)
    states = call(
        own_kernel,
        5,
        (fine,) * 4 + (coarse,) * 3,
        [scratch(4, R, C), scratch(5, R, W), scratch(6, R // 2, W)],
        smem=1,
    )(later, core, side, mk, mixing)
    *states, q3, q2, q1, cc, cf = call(
        outer_kernel,
        13,
        (fine,) * 4 + (coarse,) * 3 + (f32(Q3, C), f32(Q2, C), f32(Q1 + RG, C))
        + (f32(6, NC, W), f32(5, R, C)),
        [scratch(4, 48, C), scratch(5, 48, W)],
        smem=1,
        aliases={6 + i: i for i in range(7)},
    )(later, mk, side, mixing, up, down, *states)
    u3, qs = states[3], states[6]
    q3, q2, q1 = moved(q3, "tm", 3), moved(q2, "tm", 2), moved(q1, "tm", 1)
    inner, rest = call(
        before_kernel, 6, (f32(R * K, C), f32(R * K, C)), [scratch(R, K, C), scratch(R, K, C)]
    )(before, mixing, cf, u3, cc, mk)
    state = call(sweep_kernel, 4, coarse, [scratch(NC, K, W)])(mixing, cc, q3, q2)
    out, following = call(
        last_kernel,
        10,
        (f32(K * R, C), f32(K * R, C)),
        [scratch(NC, K, W), scratch(K * R, C), scratch(K * R, C), pltpu.SemaphoreType.DMA((2,))],
        smem=1,
        out_spec=ANY,
    )(later, mk, mixing, cc, x, state, q1, qs, rest, inner)
    return out.reshape(1, K, R, C), following.reshape(1, K, R, C)


def solution(mesh):
    in_specs = (P("tm", None, "lat", "lon"), P("lat", "lon"), P("lat", "lon"), P())
    out_specs = (P("tm", None, "lat", "lon"), P("tm", None, "lat", "lon"))
    return jax.shard_map(body, mesh=mesh, in_specs=in_specs, out_specs=out_specs, check_vma=False)
```

```python
import jax
import jax.numpy as jnp
from jax import lax
from jax.experimental import pallas as pl
from jax.experimental.pallas import tpu as pltpu
from jax.sharding import PartitionSpec as P

K = 48
R = 16
C = 128
H = 9
E = R + 2 * H
W = 2 * C
G = K // 8
SLOT = 2 * H
BASE = R - H
NC = 16
REACH = 3
RING = [*range(REACH), *range(R - REACH, R)]
SIDE = range(2, 6)
Q3, Q2, Q1, RG = 49 * 8, 42 * 8, 35 * 8, 40 * 8
LAT = H * K + 8 * H + 2 * R + 8
VMEM = pl.BlockSpec(memory_space=pltpu.VMEM)
SMEM = pl.BlockSpec(memory_space=pltpu.SMEM)
ANY = pl.BlockSpec(memory_space=pl.ANY)


def lanes(shape):
    return lax.broadcasted_iota(jnp.int32, shape, len(shape) - 1)


def shift(x, by):
    return pltpu.roll(x, by % x.shape[-1], x.ndim - 1)


def by_tile(fn, x):
    return jnp.concatenate([fn(x[:, :C]), fn(x[:, C:])], axis=1)


def pair_sum(x):
    return x + by_tile(lambda t: shift(t, -1), x)


def spread(x):
    return jnp.where(lanes(x.shape) % 2 == 0, x, shift(x, 1))


def pack_row(row):
    lane = lanes((8, C))
    out = shift(row[0:8], H)
    for g in range(1, G):
        out = jnp.where(lane < SLOT * g, out, shift(row[8 * g : 8 * g + 8], SLOT * g + H))
    return out


def unpack_row(packed):
    return jnp.concatenate([shift(packed, C - H - SLOT * g) for g in range(G)], axis=0)


def edge_kernel(x_ref, signed_ref, left_ref, right_ref, core_ref, mk_ref):
    signed = signed_ref[...]
    mask = jnp.where(signed > 0.0, 1.0, 0.0)
    mk_ref[pl.ds(0, R), :] = mask
    mk_ref[pl.ds(R, R), :] = jnp.abs(signed)
    rows = []
    for r in range(R):
        row = x_ref[pl.ds(r, K, stride=R), :] * mask[r : r + 1]
        core_ref[pl.ds(r * K, K), :] = row
        rows.append(pack_row(row))
    coefs = pack_row(jnp.concatenate([mk_ref[...], jnp.zeros((R, C), jnp.float32)], axis=0))
    rows += [coefs, coefs]
    half = len(rows) // 2
    low = lanes((8, C)) % SLOT < H
    for p in range(half):
        a, b = rows[p], rows[p + half]
        left_ref[pl.ds(8 * p, 8), :] = jnp.where(low, a, shift(b, H))
        right_ref[pl.ds(8 * p, 8), :] = jnp.where(low, shift(a, -H), b)


def halo_kernel(
    core_in, mk_ref, rl_ref, rr_ref, mix_ref,
    core_ref, top_ref, bot_ref, side_ref, fine_ref, coarse_ref,
):
    fine_ref[...] = level_matrix(mix_ref[0])
    coarse_ref[...] = level_matrix(mix_ref[1])
    half = (R + 2) // 2
    low = lanes((8, C)) % SLOT < H
    for p in range(half):
        a, b = rl_ref[pl.ds(8 * p, 8), :], rr_ref[pl.ds(8 * p, 8), :]
        side_ref[pl.ds(8 * p, 8), :] = jnp.where(low, a, shift(b, H))
        side_ref[pl.ds(8 * (p + half), 8), :] = jnp.where(low, shift(a, -H), b)
    for ref, first in ((top_ref, 0), (bot_ref, R - H)):
        ref[pl.ds(0, H * K), :] = core_in[pl.ds(first * K, H * K), :]
        ref[pl.ds(H * K, 8 * H), :] = side_ref[pl.ds(8 * first, 8 * H), :]
        ref[pl.ds(H * K + 8 * H, 2 * R), :] = mk_ref[...]
        ref[pl.ds(H * K + 8 * H + 2 * R, 8), :] = side_ref[pl.ds(8 * R, 8), :]


def split(x):
    high = x.astype(jnp.bfloat16)
    return high, (x - high.astype(jnp.float32)).astype(jnp.bfloat16)


def level_matrix(mix):
    high, low = split(mix)
    return jnp.concatenate([high, high, low], axis=1)


def levels(matrix, u):
    high, low = split(u)
    return jnp.dot(
        matrix, jnp.concatenate([high, low, high], axis=0), preferred_element_type=jnp.float32
    )


def coefficients(m, k, scale, by, out_ref):
    moves = (
        lambda a: pltpu.roll(a, 1, 0),
        lambda a: pltpu.roll(a, a.shape[0] - 1, 0),
        lambda a: shift(a, by),
        lambda a: shift(a, -by),
    )
    total = None
    for i, move in enumerate(moves):
        c = (0.5 * scale) * (k + move(k)) * (m * move(m))
        out_ref[i + 1] = c
        total = c if total is None else total + c
    out_ref[0] = m * (1.0 - total)


def fine_coarse_coefficients(mk, first, count, cf_ref, cc_ref):
    wide = lambda i: jnp.concatenate([mk[i], mk[i + 1]], axis=1)
    coefficients(wide(0), wide(2), 1.0, 1, cf_ref)
    at, after = pl.ds(first, count, stride=2), pl.ds(first + 1, count, stride=2)

    def blocks(i):
        return pair_sum(jnp.concatenate([mk[j, at] + mk[j, after] for j in (i, i + 1)], axis=1))

    wet = blocks(0)
    coefficients(
        jnp.minimum(wet, 1.0), 0.25 * blocks(2), 0.75, 2, cc_ref.at[pl.ds(0, 5)]
    )
    cc_ref[5] = 1.0 / jnp.maximum(wet, 1.0)


def stencil(coef_ref, row, by, u, north, south, matrix):
    c = [coef_ref[i, pl.ds(row, 1), :] for i in range(5)]
    near = c[0] * u + c[1] * north + c[2] * south
    side = c[3] * shift(u, by) + c[4] * shift(u, -by)
    return (near + side) + levels(matrix, u)


def step_row(src, r, coef_ref, row, by, matrix):
    return stencil(coef_ref, row, by, src[r], src[r - 1], src[r + 1], matrix)


def restrict(src, i, cc_ref, row):
    return pair_sum(src[1 + 2 * i] + src[2 + 2 * i]) * cc_ref[5, pl.ds(row, 1), :]


def own_kernel(
    later_ref, core_ref, side_ref, mk_ref, fine_mix, coarse_mix, u0, u1, u2, u3, rs, gs, qs, core_cf, mk, cf, cc
):
    for r in range(R):
        u0[H + r, :, :C] = core_ref[pl.ds(r * K, K), :]
        u0[H + r, :, C:] = unpack_row(side_ref[pl.ds(8 * r, 8), :])
    coefs = unpack_row(side_ref[pl.ds(8 * R, 8), :])
    for i in range(2):
        mk[2 * i] = mk_ref[pl.ds(i * R, R), :]
        mk[2 * i + 1] = coefs[i * R : i * R + R]
    fine_coarse_coefficients(mk, 0, R // 2, cf, cc)
    for margin, src, dst in ((1, u0, u1), (2, u1, u2), (3, u2, u3)):

        @pl.loop(margin, R - margin, unroll=R - 2 * margin)
        def _(r):
            dst[H + r] = step_row(src, H + r, cf, r, 1, fine_mix[...])

    for i in range(4, 12):
        rs[i] = restrict(u0, i, cc, i - 4)
    for i in range(5, 11):
        gs[i] = step_row(rs, i, cc, i - 4, 2, coarse_mix[...])
    for i in range(6, 10):
        qs[i] = restrict(u3, i, cc, i - 4) - later_ref[0] * gs[i]
    for i in range(5):
        core_cf[i] = cf[i, :, :C]


def put_q(q_ref, out_ref, first, count):
    even = lanes((K, W)) % 2 == 0
    for p in range(count // 2):
        odd = by_tile(lambda t: shift(t, 1), q_ref[first + 2 * p + 1])
        both = jnp.where(even, q_ref[first + 2 * p], odd)
        out_ref[pl.ds(p * K, K), :] = both[:, :C]
        out_ref[pl.ds((count // 2) * K + 8 * p, 8), :] = pack_row(both[:, C:])


def take_q(in_ref, count, write):
    for p in range(count // 2):
        core = in_ref[pl.ds(p * K, K), :]
        side = unpack_row(in_ref[pl.ds((count // 2) * K + 8 * p, 8), :])
        both = jnp.concatenate([core, side], axis=1)
        write(2 * p, both)
        write(2 * p + 1, by_tile(lambda t: shift(t, -1), both))


def put_ring(src, out_ref):
    for i, r in enumerate(RING):
        out_ref[pl.ds(Q1 + i * K, K), :] = src[H + r, :, :C]
    at = lanes((8, C)) % SLOT
    for i, r in enumerate(SIDE):
        a, b, c = (pack_row(src[H + r + d, :, :C]) for d in (0, 4, 8))
        both = jnp.where(at < 2 * REACH, shift(a, -2 * REACH), b)
        both = jnp.where(at < 4 * REACH, both, shift(c, 2 * REACH))
        out_ref[pl.ds(Q1 + len(RING) * K + 8 * i, 8), :] = both


def take_ring(in_ref, inner_ref):
    rows = {r: in_ref[pl.ds(Q1 + i * K, K), :] for i, r in enumerate(RING)}
    lane = lanes((K, C))
    inside = (lane >= REACH) & (lane < C - REACH)
    for i, r in enumerate(SIDE):
        packed = in_ref[pl.ds(Q1 + len(RING) * K + 8 * i, 8), :]
        for d, by in ((0, 2 * REACH), (4, 0), (8, -2 * REACH)):
            if r + d not in rows:
                ends = unpack_row(shift(packed, by))
                rows[r + d] = jnp.where(inside, inner_ref[pl.ds((r + d) * K, K), :], ends)
    return [rows[r] for r in range(R)]


def outer_rows(
    upper, later_ref, mk_ref, side_ref, fine_mix, coarse_mix, halo_ref, states, cc_out, mk, cf, cc
):
    u0, u1, u2, u3, rs, gs, qs = states
    mk[...] = jnp.zeros_like(mk)
    first = 0 if upper else H + R
    for i in range(H):
        u0[first + i, :, :C] = halo_ref[pl.ds(i * K, K), :]
        u0[first + i, :, C:] = unpack_row(halo_ref[pl.ds(H * K + 8 * i, 8), :])
    at = H * K + 8 * H
    for j, ref, at, side, side_at in (
        (0 if upper else 2, halo_ref, at, halo_ref, at + 2 * R),
        (1, mk_ref, 0, side_ref, 8 * R),
    ):
        coefs = unpack_row(side[pl.ds(side_at, 8), :])
        for i in range(2):
            mk[2 * i, pl.ds(j * R, R), :] = ref[pl.ds(at + i * R, R), :]
            mk[2 * i + 1, pl.ds(j * R, R), :] = coefs[i * R : i * R + R]
    fine_coarse_coefficients(mk, R - 8, NC, cf, cc)
    for margin, src, dst in ((1, u0, u1), (2, u1, u2), (3, u2, u3)):

        @pl.loop(0, H, unroll=H)
        def _(i):
            r = margin + i if upper else E - 1 - margin - i
            dst[r] = step_row(src, r, cf, r + BASE, 1, fine_mix[...])

    mirror = lambda rows: rows if upper else [NC - 1 - i for i in rows]
    for i in mirror([0, 1, 2, 3]):
        rs[i] = restrict(u0, i, cc, i)
    for i in mirror([1, 2, 3, 4]):
        gs[i] = step_row(rs, i, cc, i, 2, coarse_mix[...])
    for i in mirror([1, 2, 3, 4, 5]):
        qs[i] = restrict(u3, i, cc, i) - later_ref[0] * gs[i]
    half = pl.ds(0 if upper else NC // 2, NC // 2)
    for i in range(6):
        cc_out[i, half, :] = cc[i, half, :]


def upper_kernel(*refs):
    *ins, mk, cf, cc = refs
    outer_rows(True, *ins[:6], ins[13:20], ins[20], mk, cf, cc)


def lower_kernel(*refs):
    *ins, q3_ref, q2_ref, q1_ref, mk, cf, cc = refs
    states = ins[14:21]
    outer_rows(False, *ins[:6], states, ins[21], mk, cf, cc)
    u3, qs = states[3], states[6]
    put_q(qs, q3_ref, 1, 14)
    put_q(qs, q2_ref, 2, 12)
    put_q(qs, q1_ref, 3, 10)
    put_ring(u3, q1_ref)


def before_kernel(core_ref, fine_mix, cf_ref, u3, cc_ref, mk_ref, inner_ref, rest_ref, ua, ub):
    for r in range(R):
        ua[r] = core_ref[pl.ds(r * K, K), :]
    for margin, src, dst in ((1, ua, ub), (2, ub, ua), (3, ua, None)):
        for r in range(margin, R - margin):
            value = step_row(src, r, cf_ref, r, 1, fine_mix[...])
            if dst is None:
                inner_ref[pl.ds(r * K, K), :] = value
            else:
                dst[r] = value
    for r in RING:
        inner_ref[pl.ds(r * K, K), :] = jnp.zeros((K, C), jnp.float32)
    for i in range(R // 2):
        pair = [u3[H + r, :, :C] for r in (2 * i, 2 * i + 1)]
        fc = spread(block_mean(pair, cc_ref, i))
        for r, value in zip((2 * i, 2 * i + 1), pair):
            rest_ref[pl.ds(r * K, K), :] = value - mk_ref[pl.ds(r, 1), :] * fc


def block_mean(pair, cc_ref, i):
    total = pair[0] + pair[1]
    return (total + shift(total, -1)) * cc_ref[5, 4 + i : 5 + i, :C]


def near_kernel(q1_ref, inner_ref, cc_ref, mk_ref, a, base_ref):
    take_q(q1_ref, 10, lambda i, value: a.__setitem__(3 + i, value))
    rows = take_ring(q1_ref, inner_ref)
    for i in range(R // 2):
        pair = rows[2 * i], rows[2 * i + 1]
        fc = spread(block_mean(pair, cc_ref, i))
        for r, value in zip((2 * i, 2 * i + 1), pair):
            base_ref[pl.ds(r * K, K), :] = value - mk_ref[pl.ds(r, 1), :] * fc


def far_kernel(coarse_mix, cc_ref, q3_ref, b, a):
    take_q(q3_ref, 14, lambda i, value: a.__setitem__(1 + i, value))
    for i in range(2, 14):
        b[i] = step_row(a, i, cc_ref, i, 2, coarse_mix[...])


def last_kernel(
    later_ref, mk_ref, coarse_mix, cc_ref, x_ref, far, near, q2_ref, qs, rest_ref, base_ref,
    out_hbm, next_hbm, a, b, out_ref, next_ref, sems,
):
    take_q(q2_ref, 12, lambda i, value: b.__setitem__(2 + i, far[2 + i] + value))
    for i in range(3, 13):
        a[i] = near[i] + step_row(b, i, cc_ref, i, 2, coarse_mix[...])
    first = later_ref[0] == 0.0

    def put(ref, from_ref, i, value):
        value = spread(value)
        for r in (2 * i, 2 * i + 1):
            total = from_ref[pl.ds(r * K, K), :] + mk_ref[pl.ds(r, 1), :] * value
            ref[pl.ds(r, K, stride=R), :] = total

    @pl.when(first)
    def _():
        next_ref[...] = x_ref[...]

    @pl.when(jnp.logical_not(first))
    def _():
        for i in range(R // 2):
            put(next_ref, base_ref, i, a[4 + i, :, :C])

    next_copy = pltpu.make_async_copy(next_ref, next_hbm, sems.at[0])
    next_copy.start()
    for i in range(R // 2):
        z = qs[4 + i] + step_row(a, 4 + i, cc_ref, 4 + i, 2, coarse_mix[...])
        put(out_ref, rest_ref, i, z[:, :C])
    out_copy = pltpu.make_async_copy(out_ref, out_hbm, sems.at[1])
    out_copy.start()
    next_copy.wait()
    out_copy.wait()


def f32(*shape):
    return jax.ShapeDtypeStruct(shape, jnp.float32)


def scratch(*shape):
    return pltpu.VMEM(shape, jnp.float32)


def call(kernel, n_in, outs, scratches=(), smem=0, aliases=None, out_spec=VMEM):
    return pl.pallas_call(
        kernel,
        out_shape=outs,
        in_specs=[SMEM] * smem + [VMEM] * (n_in - smem),
        out_specs=jax.tree.map(lambda _: out_spec, outs),
        scratch_shapes=list(scratches),
        input_output_aliases=aliases or {},
        compiler_params=pltpu.CompilerParams(vmem_limit_bytes=40 * 1024 * 1024),
    )


def moved(value, axis, by, wrap=False):
    n = lax.axis_size(axis)
    pairs = [(i, (i + by) % n) for i in range(n) if wrap or 0 <= i + by < n]
    return lax.ppermute(value, axis, pairs)


def body(start, wet, kappa, mixing):
    x = start.reshape(K * R, C)
    later = (lax.axis_index("tm") > 0).astype(jnp.float32).reshape(1)
    mixing = mixing[None] * jnp.array([1.0, 3.0], jnp.float32)[:, None, None]
    lon = (R + 2) * 4
    left, right, core, mk = call(
        edge_kernel, 2, (f32(lon, C), f32(lon, C), f32(R * K, C), f32(2 * R, C))
    )(x, jnp.where(wet > 0, kappa, -kappa))
    from_left = moved(left, "lon", 1, True)
    from_right = moved(right, "lon", -1, True)
    matrix = jax.ShapeDtypeStruct((K, 3 * K), jnp.bfloat16)
    core, top, bottom, side, fine_mix, coarse_mix = call(
        halo_kernel,
        5,
        (f32(R * K, C), f32(LAT, C), f32(LAT, C), f32(8 * (R + 2), C), matrix, matrix),
        aliases={0: 0},
    )(core, mk, from_left, from_right, mixing)
    down = moved(top, "lat", -1)
    up = moved(bottom, "lat", 1)
    before = moved(core, "tm", 1)
    fine, coarse = f32(E, K, W), f32(NC, K, W)
    shapes = (fine,) * 4 + (coarse,) * 3
    *states, cf = call(
        own_kernel,
        6,
        shapes + (f32(5, R, C),),
        [scratch(4, R, C), scratch(5, R, W), scratch(6, R // 2, W)],
        smem=1,
    )(later, core, side, mk, fine_mix, coarse_mix)
    parts = [scratch(4, 48, C), scratch(5, 48, W), scratch(6, NC, W)]
    coefs = f32(6, NC, W)
    states = call(
        upper_kernel, 13, shapes + (coefs,), parts, smem=1, aliases={6 + i: i for i in range(7)}
    )(later, mk, side, fine_mix, coarse_mix, up, *states)
    *states, cc, q3, q2, q1 = call(
        lower_kernel,
        14,
        shapes + (coefs, f32(Q3, C), f32(Q2, C), f32(Q1 + RG, C)),
        parts,
        smem=1,
        aliases={6 + i: i for i in range(8)},
    )(later, mk, side, fine_mix, coarse_mix, down, *states)
    u3, qs = states[3], states[6]
    q3, q2, q1 = moved(q3, "tm", 3), moved(q2, "tm", 2), moved(q1, "tm", 1)
    inner, rest = call(
        before_kernel, 6, (f32(R * K, C), f32(R * K, C)), [scratch(R, K, C), scratch(R, K, C)]
    )(before, fine_mix, cf, u3, cc, mk)
    near, base = call(near_kernel, 4, (coarse, f32(R * K, C)))(q1, inner, cc, mk)
    far = call(far_kernel, 3, coarse, [scratch(NC, K, W)])(coarse_mix, cc, q3)
    out, following = call(
        last_kernel,
        11,
        (f32(K * R, C), f32(K * R, C)),
        [scratch(NC, K, W)] * 2 + [scratch(K * R, C)] * 2 + [pltpu.SemaphoreType.DMA((2,))],
        smem=1,
        out_spec=ANY,
    )(later, mk, coarse_mix, cc, x, far, near, q2, qs, rest, base)
    return out.reshape(1, K, R, C), following.reshape(1, K, R, C)


def solution(mesh):
    in_specs = (P("tm", None, "lat", "lon"), P("lat", "lon"), P("lat", "lon"), P())
    out_specs = (P("tm", None, "lat", "lon"), P("tm", None, "lat", "lon"))
    return jax.shard_map(body, mesh=mesh, in_specs=in_specs, out_specs=out_specs, check_vma=False)
```

```python
import jax
import jax.numpy as jnp
from jax import lax
from jax.experimental import pallas as pl
from jax.experimental.pallas import tpu as pltpu
from jax.sharding import PartitionSpec as P

K = 48
R = 16
C = 128
H = 9
E = R + 2 * H
W = 2 * C
G = K // 8
SLOT = 2 * H
BASE = R - H
NC = 16
REACH = 3
RING = [*range(REACH), *range(R - REACH, R)]
SIDE = range(2, 6)
Q3, Q2, Q1, RG = 49 * 8, 39 * 8, 32 * 8, 40 * 8
LAT = H * K + 8 * H + 2 * R + 8
VMEM = pl.BlockSpec(memory_space=pltpu.VMEM)
SMEM = pl.BlockSpec(memory_space=pltpu.SMEM)
ANY = pl.BlockSpec(memory_space=pl.ANY)


def lanes(shape):
    return lax.broadcasted_iota(jnp.int32, shape, len(shape) - 1)


def shift(x, by):
    return pltpu.roll(x, by % x.shape[-1], x.ndim - 1)


def by_tile(fn, x):
    return jnp.concatenate([fn(x[:, :C]), fn(x[:, C:])], axis=1)


def pair_sum(x):
    return x + by_tile(lambda t: shift(t, -1), x)


def spread(x):
    return jnp.where(lanes(x.shape) % 2 == 0, x, shift(x, 1))


def pack_row(row):
    lane = lanes((8, C))
    out = shift(row[0:8], H)
    for g in range(1, G):
        out = jnp.where(lane < SLOT * g, out, shift(row[8 * g : 8 * g + 8], SLOT * g + H))
    return out


def unpack_row(packed):
    return jnp.concatenate([shift(packed, C - H - SLOT * g) for g in range(G)], axis=0)


def edge_kernel(x_ref, signed_ref, left_ref, right_ref, core_ref, mk_ref):
    signed = signed_ref[...]
    mask = jnp.where(signed > 0.0, 1.0, 0.0)
    mk_ref[pl.ds(0, R), :] = mask
    mk_ref[pl.ds(R, R), :] = jnp.abs(signed)
    rows = []
    for r in range(R):
        row = x_ref[pl.ds(r, K, stride=R), :] * mask[r : r + 1]
        core_ref[pl.ds(r * K, K), :] = row
        rows.append(pack_row(row))
    coefs = pack_row(jnp.concatenate([mk_ref[...], jnp.zeros((R, C), jnp.float32)], axis=0))
    rows += [coefs, coefs]
    half = len(rows) // 2
    low = lanes((8, C)) % SLOT < H
    for p in range(half):
        a, b = rows[p], rows[p + half]
        left_ref[pl.ds(8 * p, 8), :] = jnp.where(low, a, shift(b, H))
        right_ref[pl.ds(8 * p, 8), :] = jnp.where(low, shift(a, -H), b)


def halo_kernel(
    core_in, mk_ref, rl_ref, rr_ref, mix_ref,
    core_ref, top_ref, bot_ref, side_ref, fine_ref, coarse_ref,
):
    fine_ref[...] = level_matrix(mix_ref[0])
    coarse_ref[...] = level_matrix(mix_ref[1])
    half = (R + 2) // 2
    low = lanes((8, C)) % SLOT < H
    for p in range(half):
        a, b = rl_ref[pl.ds(8 * p, 8), :], rr_ref[pl.ds(8 * p, 8), :]
        side_ref[pl.ds(8 * p, 8), :] = jnp.where(low, a, shift(b, H))
        side_ref[pl.ds(8 * (p + half), 8), :] = jnp.where(low, shift(a, -H), b)
    for ref, first in ((top_ref, 0), (bot_ref, R - H)):
        ref[pl.ds(0, H * K), :] = core_in[pl.ds(first * K, H * K), :]
        ref[pl.ds(H * K, 8 * H), :] = side_ref[pl.ds(8 * first, 8 * H), :]
        ref[pl.ds(H * K + 8 * H, 2 * R), :] = mk_ref[...]
        ref[pl.ds(H * K + 8 * H + 2 * R, 8), :] = side_ref[pl.ds(8 * R, 8), :]


def split(x):
    high = x.astype(jnp.bfloat16)
    return high, (x - high.astype(jnp.float32)).astype(jnp.bfloat16)


def level_matrix(mix):
    high, low = split(mix)
    return jnp.concatenate([high, high, low], axis=1)


def levels(matrix, u):
    high, low = split(u)
    return jnp.dot(
        matrix, jnp.concatenate([high, low, high], axis=0), preferred_element_type=jnp.float32
    )


def coefficients(m, k, scale, by, out_ref):
    moves = (
        lambda a: pltpu.roll(a, 1, 0),
        lambda a: pltpu.roll(a, a.shape[0] - 1, 0),
        lambda a: shift(a, by),
        lambda a: shift(a, -by),
    )
    total = None
    for i, move in enumerate(moves):
        c = (0.5 * scale) * (k + move(k)) * (m * move(m))
        out_ref[i + 1] = c
        total = c if total is None else total + c
    out_ref[0] = m * (1.0 - total)


def fine_coarse_coefficients(mk, first, count, cf_ref, cc_ref):
    wide = lambda i: jnp.concatenate([mk[i], mk[i + 1]], axis=1)
    coefficients(wide(0), wide(2), 1.0, 1, cf_ref)
    at, after = pl.ds(first, count, stride=2), pl.ds(first + 1, count, stride=2)

    def blocks(i):
        return pair_sum(jnp.concatenate([mk[j, at] + mk[j, after] for j in (i, i + 1)], axis=1))

    wet = blocks(0)
    coefficients(
        jnp.minimum(wet, 1.0), 0.25 * blocks(2), 0.75, 2, cc_ref.at[pl.ds(0, 5)]
    )
    cc_ref[5] = 1.0 / jnp.maximum(wet, 1.0)


def stencil(coef_ref, row, by, u, north, south, matrix):
    c = [coef_ref[i, pl.ds(row, 1), :] for i in range(5)]
    near = c[0] * u + c[1] * north + c[2] * south
    side = c[3] * shift(u, by) + c[4] * shift(u, -by)
    return (near + side) + levels(matrix, u)


def step_row(src, r, coef_ref, row, by, matrix):
    return stencil(coef_ref, row, by, src[r], src[r - 1], src[r + 1], matrix)


def restrict(src, i, cc_ref, row):
    return pair_sum(src[1 + 2 * i] + src[2 + 2 * i]) * cc_ref[5, pl.ds(row, 1), :]


def own_kernel(
    later_ref, core_ref, side_ref, mk_ref, fine_mix, coarse_mix, u0, u1, u2, u3, rs, gs, qs, core_cf, mk, cf, cc
):
    for r in range(R):
        u0[H + r, :, :C] = core_ref[pl.ds(r * K, K), :]
        u0[H + r, :, C:] = unpack_row(side_ref[pl.ds(8 * r, 8), :])
    coefs = unpack_row(side_ref[pl.ds(8 * R, 8), :])
    for i in range(2):
        mk[2 * i] = mk_ref[pl.ds(i * R, R), :]
        mk[2 * i + 1] = coefs[i * R : i * R + R]
    fine_coarse_coefficients(mk, 0, R // 2, cf, cc)
    for margin, src, dst in ((1, u0, u1), (2, u1, u2), (3, u2, u3)):

        @pl.loop(margin, R - margin, unroll=R - 2 * margin)
        def _(r):
            dst[H + r] = step_row(src, H + r, cf, r, 1, fine_mix[...])

    for i in range(4, 12):
        rs[i] = restrict(u0, i, cc, i - 4)
    for i in range(5, 11):
        gs[i] = step_row(rs, i, cc, i - 4, 2, coarse_mix[...])
    for i in range(6, 10):
        qs[i] = restrict(u3, i, cc, i - 4) - later_ref[0] * gs[i]
    for i in range(5):
        core_cf[i] = cf[i, :, :C]


PAIRS3 = [(i, i + 1) for i in range(1, 15, 2)]
PAIRS2 = [(2, 13), *PAIRS3[1:6]]
PAIRS1 = PAIRS3[1:6]


def join(qs, pair):
    even = lanes((K, W)) % 2 == 0
    return jnp.where(even, qs[pair[0]], by_tile(lambda t: shift(t, 1), qs[pair[1]]))


def put_q3(qs, out_ref, indices):
    for p in indices:
        both = join(qs, PAIRS3[p])
        out_ref[pl.ds(p * K, K), :] = both[:, :C]
        out_ref[pl.ds(7 * K + 8 * p, 8), :] = pack_row(both[:, C:])


def ends3(q3_ref, p):
    return q3_ref[pl.ds(7 * K + 8 * p, 8), :]


def put_q2(qs, q3_ref, out_ref):
    both = join(qs, PAIRS2[0])
    out_ref[pl.ds(0, K), :] = both[:, :C]
    out_ref[pl.ds(K, 5 * K), :] = q3_ref[pl.ds(K, 5 * K), :]
    ends = [pack_row(both[:, C:])] + [ends3(q3_ref, p) for p in range(1, 6)]
    low = lanes((8, C)) % SLOT < H
    for j in range(3):
        both = jnp.where(low, shift(ends[j], -5), shift(ends[j + 3], 4))
        out_ref[pl.ds(6 * K + 8 * j, 8), :] = both


def put_q1(q3_ref, out_ref):
    out_ref[pl.ds(0, 5 * K), :] = q3_ref[pl.ds(K, 5 * K), :]
    ends = [ends3(q3_ref, p) for p in range(1, 6)]
    at = lanes((8, C)) % SLOT
    both = shift(ends[3], 5)
    for k in (2, 1, 0):
        both = jnp.where(at < 4 * k + 4, shift(ends[k], 4 * k - 7), both)
    out_ref[pl.ds(5 * K, 8), :] = both
    out_ref[pl.ds(5 * K + 8, 8), :] = ends[4]


def take_q(in_ref, pairs, write):
    for p, (first, second) in enumerate(pairs):
        n = len(pairs)
        ends = lambda j: in_ref[pl.ds(n * K + 8 * j, 8), :]
        if n == 7:
            packed = ends(p)
        elif n == 6:
            packed = shift(ends(p % 3), 5 if p < 3 else -4)
        else:
            packed = shift(ends(0), 7 - 4 * p) if p < 4 else ends(1)
        both = jnp.concatenate([in_ref[pl.ds(p * K, K), :], unpack_row(packed)], axis=1)
        write(first, both)
        write(second, by_tile(lambda t: shift(t, -1), both))


def put_ring(src, out_ref):
    for i, r in enumerate(RING):
        out_ref[pl.ds(Q1 + i * K, K), :] = src[H + r, :, :C]
    at = lanes((8, C)) % SLOT
    for i, r in enumerate(SIDE):
        a, b, c = (pack_row(src[H + r + d, :, :C]) for d in (0, 4, 8))
        both = jnp.where(at < 2 * REACH, shift(a, -2 * REACH), b)
        both = jnp.where(at < 4 * REACH, both, shift(c, 2 * REACH))
        out_ref[pl.ds(Q1 + len(RING) * K + 8 * i, 8), :] = both


def take_ring(in_ref, inner_ref):
    rows = {r: in_ref[pl.ds(Q1 + i * K, K), :] for i, r in enumerate(RING)}
    lane = lanes((K, C))
    inside = (lane >= REACH) & (lane < C - REACH)
    for i, r in enumerate(SIDE):
        packed = in_ref[pl.ds(Q1 + len(RING) * K + 8 * i, 8), :]
        for d, by in ((0, 2 * REACH), (4, 0), (8, -2 * REACH)):
            if r + d not in rows:
                ends = unpack_row(shift(packed, by))
                rows[r + d] = jnp.where(inside, inner_ref[pl.ds((r + d) * K, K), :], ends)
    return [rows[r] for r in range(R)]


def outer_rows(
    upper, later_ref, mk_ref, side_ref, fine_mix, coarse_mix, halo_ref, states, cc_out, mk, cf, cc
):
    u0, u1, u2, u3, rs, gs, qs = states
    mk[...] = jnp.zeros_like(mk)
    first = 0 if upper else H + R
    for i in range(H):
        u0[first + i, :, :C] = halo_ref[pl.ds(i * K, K), :]
        u0[first + i, :, C:] = unpack_row(halo_ref[pl.ds(H * K + 8 * i, 8), :])
    at = H * K + 8 * H
    for j, ref, at, side, side_at in (
        (0 if upper else 2, halo_ref, at, halo_ref, at + 2 * R),
        (1, mk_ref, 0, side_ref, 8 * R),
    ):
        coefs = unpack_row(side[pl.ds(side_at, 8), :])
        for i in range(2):
            mk[2 * i, pl.ds(j * R, R), :] = ref[pl.ds(at + i * R, R), :]
            mk[2 * i + 1, pl.ds(j * R, R), :] = coefs[i * R : i * R + R]
    fine_coarse_coefficients(mk, R - 8, NC, cf, cc)
    for margin, src, dst in ((1, u0, u1), (2, u1, u2), (3, u2, u3)):

        @pl.loop(0, H, unroll=H)
        def _(i):
            r = margin + i if upper else E - 1 - margin - i
            dst[r] = step_row(src, r, cf, r + BASE, 1, fine_mix[...])

    mirror = lambda rows: rows if upper else [NC - 1 - i for i in rows]
    for i in mirror([0, 1, 2, 3]):
        rs[i] = restrict(u0, i, cc, i)
    for i in mirror([1, 2, 3, 4]):
        gs[i] = step_row(rs, i, cc, i, 2, coarse_mix[...])
    for i in mirror([1, 2, 3, 4, 5]):
        qs[i] = restrict(u3, i, cc, i) - later_ref[0] * gs[i]
    half = pl.ds(0 if upper else NC // 2, NC // 2)
    for i in range(6):
        cc_out[i, half, :] = cc[i, half, :]


def upper_kernel(*refs):
    *ins, mk, cf, cc = refs
    states, cc_out, q3_ref = ins[13:20], ins[20], ins[21]
    outer_rows(True, *ins[:6], states, cc_out, mk, cf, cc)
    put_q3(states[6], q3_ref, range(4))


def lower_kernel(*refs):
    *ins, mk, cf, cc = refs
    states, cc_out, q3_ref, q2_ref = ins[15:22], ins[22], ins[23], ins[24]
    outer_rows(False, *ins[:6], states, cc_out, mk, cf, cc)
    put_q3(states[6], q3_ref, range(4, 7))
    put_q2(states[6], q3_ref, q2_ref)


def near_message_kernel(u3, q3_ref, out_ref):
    put_q1(q3_ref, out_ref)
    put_ring(u3, out_ref)


def before_kernel(core_ref, fine_mix, cf_ref, u3, cc_ref, mk_ref, inner_ref, rest_ref, ua, ub):
    for r in range(R):
        ua[r] = core_ref[pl.ds(r * K, K), :]
    for margin, src, dst in ((1, ua, ub), (2, ub, ua), (3, ua, None)):
        for r in range(margin, R - margin):
            value = step_row(src, r, cf_ref, r, 1, fine_mix[...])
            if dst is None:
                inner_ref[pl.ds(r * K, K), :] = value
            else:
                dst[r] = value
    for r in RING:
        inner_ref[pl.ds(r * K, K), :] = jnp.zeros((K, C), jnp.float32)
    for i in range(R // 2):
        pair = [u3[H + r, :, :C] for r in (2 * i, 2 * i + 1)]
        fc = spread(block_mean(pair, cc_ref, i))
        for r, value in zip((2 * i, 2 * i + 1), pair):
            rest_ref[pl.ds(r * K, K), :] = value - mk_ref[pl.ds(r, 1), :] * fc


def block_mean(pair, cc_ref, i):
    total = pair[0] + pair[1]
    return (total + shift(total, -1)) * cc_ref[5, 4 + i : 5 + i, :C]


def near_kernel(q1_ref, inner_ref, cc_ref, mk_ref, a, base_ref):
    take_q(q1_ref, PAIRS1, lambda i, value: a.__setitem__(i, value))
    rows = take_ring(q1_ref, inner_ref)
    for i in range(R // 2):
        pair = rows[2 * i], rows[2 * i + 1]
        fc = spread(block_mean(pair, cc_ref, i))
        for r, value in zip((2 * i, 2 * i + 1), pair):
            base_ref[pl.ds(r * K, K), :] = value - mk_ref[pl.ds(r, 1), :] * fc


def far_kernel(coarse_mix, cc_ref, q3_ref, _, b, a):
    take_q(q3_ref, PAIRS3, lambda i, value: a.__setitem__(i, value))
    for i in range(2, 14):
        b[i] = step_row(a, i, cc_ref, i, 2, coarse_mix[...])


def last_kernel(
    later_ref, mk_ref, coarse_mix, cc_ref, x_ref, far, near, q2_ref, qs, rest_ref, base_ref,
    out_hbm, next_hbm, a, b, out_ref, next_ref, sems,
):
    take_q(q2_ref, PAIRS2, lambda i, value: b.__setitem__(i, far[i] + value))
    for i in range(3, 13):
        a[i] = near[i] + step_row(b, i, cc_ref, i, 2, coarse_mix[...])
    first = later_ref[0] == 0.0

    def put(ref, from_ref, i, value):
        value = spread(value)
        for r in (2 * i, 2 * i + 1):
            total = from_ref[pl.ds(r * K, K), :] + mk_ref[pl.ds(r, 1), :] * value
            ref[pl.ds(r, K, stride=R), :] = total

    @pl.when(first)
    def _():
        next_ref[...] = x_ref[...]

    @pl.when(jnp.logical_not(first))
    def _():
        for i in range(R // 2):
            put(next_ref, base_ref, i, a[4 + i, :, :C])

    next_copy = pltpu.make_async_copy(next_ref, next_hbm, sems.at[0])
    next_copy.start()
    for i in range(R // 2):
        z = qs[4 + i] + step_row(a, 4 + i, cc_ref, 4 + i, 2, coarse_mix[...])
        put(out_ref, rest_ref, i, z[:, :C])
    out_copy = pltpu.make_async_copy(out_ref, out_hbm, sems.at[1])
    out_copy.start()
    next_copy.wait()
    out_copy.wait()


def f32(*shape):
    return jax.ShapeDtypeStruct(shape, jnp.float32)


def scratch(*shape):
    return pltpu.VMEM(shape, jnp.float32)


def call(kernel, n_in, outs, scratches=(), smem=0, aliases=None, out_spec=VMEM):
    return pl.pallas_call(
        kernel,
        out_shape=outs,
        in_specs=[SMEM] * smem + [VMEM] * (n_in - smem),
        out_specs=jax.tree.map(lambda _: out_spec, outs),
        scratch_shapes=list(scratches),
        input_output_aliases=aliases or {},
        compiler_params=pltpu.CompilerParams(vmem_limit_bytes=40 * 1024 * 1024),
    )


def moved(value, axis, by, wrap=False):
    n = lax.axis_size(axis)
    pairs = [(i, (i + by) % n) for i in range(n) if wrap or 0 <= i + by < n]
    return lax.ppermute(value, axis, pairs)


def body(start, wet, kappa, mixing):
    x = start.reshape(K * R, C)
    later = (lax.axis_index("tm") > 0).astype(jnp.float32).reshape(1)
    mixing = mixing[None] * jnp.array([1.0, 3.0], jnp.float32)[:, None, None]
    lon = (R + 2) * 4
    left, right, core, mk = call(
        edge_kernel, 2, (f32(lon, C), f32(lon, C), f32(R * K, C), f32(2 * R, C))
    )(x, jnp.where(wet > 0, kappa, -kappa))
    from_left = moved(left, "lon", 1, True)
    from_right = moved(right, "lon", -1, True)
    matrix = jax.ShapeDtypeStruct((K, 3 * K), jnp.bfloat16)
    core, top, bottom, side, fine_mix, coarse_mix = call(
        halo_kernel,
        5,
        (f32(R * K, C), f32(LAT, C), f32(LAT, C), f32(8 * (R + 2), C), matrix, matrix),
        aliases={0: 0},
    )(core, mk, from_left, from_right, mixing)
    down = moved(top, "lat", -1)
    up = moved(bottom, "lat", 1)
    before = moved(core, "tm", 1)
    fine, coarse = f32(E, K, W), f32(NC, K, W)
    shapes = (fine,) * 4 + (coarse,) * 3
    *states, cf = call(
        own_kernel,
        6,
        shapes + (f32(5, R, C),),
        [scratch(4, R, C), scratch(5, R, W), scratch(6, R // 2, W)],
        smem=1,
    )(later, core, side, mk, fine_mix, coarse_mix)
    parts = [scratch(4, 48, C), scratch(5, 48, W), scratch(6, NC, W)]
    coefs = f32(6, NC, W)
    states = call(
        upper_kernel,
        13,
        shapes + (coefs, f32(Q3, C)),
        parts,
        smem=1,
        aliases={6 + i: i for i in range(7)},
    )(later, mk, side, fine_mix, coarse_mix, up, *states)
    *states, cc, q3, q2 = call(
        lower_kernel,
        15,
        shapes + (coefs, f32(Q3, C), f32(Q2, C)),
        parts,
        smem=1,
        aliases={6 + i: i for i in range(9)},
    )(later, mk, side, fine_mix, coarse_mix, down, *states)
    u3, qs = states[3], states[6]
    q1 = call(near_message_kernel, 2, f32(Q1 + RG, C))(u3, q3)
    q3, q2, q1 = moved(q3, "tm", 3), moved(q2, "tm", 2), moved(q1, "tm", 1)
    inner, rest = call(
        before_kernel, 6, (f32(R * K, C), f32(R * K, C)), [scratch(R, K, C), scratch(R, K, C)]
    )(before, fine_mix, cf, u3, cc, mk)
    near, base = call(near_kernel, 4, (coarse, f32(R * K, C)))(q1, inner, cc, mk)
    far = call(far_kernel, 4, coarse, [scratch(NC, K, W)])(coarse_mix, cc, q3, near)
    out, following = call(
        last_kernel,
        11,
        (f32(K * R, C), f32(K * R, C)),
        [scratch(NC, K, W)] * 2 + [scratch(K * R, C)] * 2 + [pltpu.SemaphoreType.DMA((2,))],
        smem=1,
        out_spec=ANY,
    )(later, mk, coarse_mix, cc, x, far, near, q2, qs, rest, base)
    return out.reshape(1, K, R, C), following.reshape(1, K, R, C)


def solution(mesh):
    in_specs = (P("tm", None, "lat", "lon"), P("lat", "lon"), P("lat", "lon"), P())
    out_specs = (P("tm", None, "lat", "lon"), P("tm", None, "lat", "lon"))
    return jax.shard_map(body, mesh=mesh, in_specs=in_specs, out_specs=out_specs, check_vma=False)
```

```python
import jax
import jax.numpy as jnp
from jax import lax
from jax.experimental import pallas as pl
from jax.experimental.pallas import tpu as pltpu
from jax.sharding import PartitionSpec as P

K = 48
R = 16
C = 128
H = 9
E = R + 2 * H
W = 2 * C
G = K // 8
SLOT = 2 * H
BASE = R - H
NC = 16
REACH = 3
RING = [*range(REACH), *range(R - REACH, R)]
SIDE = range(2, 6)
Q3, Q2, Q1, RG = 49 * 8, 39 * 8, 21 * 8, 40 * 8
HALF = (H - 1) // 2
LAT = H * K + 8 * HALF + 2 * R + 8
VMEM = pl.BlockSpec(memory_space=pltpu.VMEM)
SMEM = pl.BlockSpec(memory_space=pltpu.SMEM)
ANY = pl.BlockSpec(memory_space=pl.ANY)


def lanes(shape):
    return lax.broadcasted_iota(jnp.int32, shape, len(shape) - 1)


def shift(x, by):
    return pltpu.roll(x, by % x.shape[-1], x.ndim - 1)


def by_tile(fn, x):
    return jnp.concatenate([fn(x[:, :C]), fn(x[:, C:])], axis=1)


def pair_sum(x):
    return x + by_tile(lambda t: shift(t, -1), x)


def spread(x):
    return jnp.where(lanes(x.shape) % 2 == 0, x, shift(x, 1))


def pack_row(row):
    lane = lanes((8, C))
    out = shift(row[0:8], H)
    for g in range(1, G):
        out = jnp.where(lane < SLOT * g, out, shift(row[8 * g : 8 * g + 8], SLOT * g + H))
    return out


def unpack_row(packed):
    return jnp.concatenate([shift(packed, C - H - SLOT * g) for g in range(G)], axis=0)


def edge_kernel(x_ref, signed_ref, left_ref, right_ref, core_ref, mk_ref):
    signed = signed_ref[...]
    mask = jnp.where(signed > 0.0, 1.0, 0.0)
    mk_ref[pl.ds(0, R), :] = mask
    mk_ref[pl.ds(R, R), :] = jnp.abs(signed)
    rows = []
    for r in range(R):
        row = x_ref[pl.ds(r, K, stride=R), :] * mask[r : r + 1]
        core_ref[pl.ds(r * K, K), :] = row
        rows.append(pack_row(row))
    coefs = pack_row(jnp.concatenate([mk_ref[...], jnp.zeros((R, C), jnp.float32)], axis=0))
    rows += [coefs, coefs]
    half = len(rows) // 2
    low = lanes((8, C)) % SLOT < H
    for p in range(half):
        a, b = rows[p], rows[p + half]
        left_ref[pl.ds(8 * p, 8), :] = jnp.where(low, a, shift(b, H))
        right_ref[pl.ds(8 * p, 8), :] = jnp.where(low, shift(a, -H), b)


def corner_rows(j, first_rows):
    d = j + 1
    place = (lambda k: k - 1) if first_rows else (lambda k: H - k)
    return d, place(d), place(H - d)


def corner_ends(halo_ref, first_rows):
    low = lanes((8, C)) % SLOT < H
    ends = [None] * H
    for j in range(HALF):
        d, near, far = corner_rows(j, first_rows)
        both = halo_ref[pl.ds(H * K + 8 * j, 8), :]
        ends[near] = both
        ends[far] = jnp.where(low, shift(both, H - d), shift(both, d - H))
    return ends


def halo_kernel(
    core_in, mk_ref, rl_ref, rr_ref, mix_ref,
    core_ref, top_ref, bot_ref, side_ref, fine_ref, coarse_ref,
):
    fine_ref[...] = level_matrix(mix_ref[0])
    coarse_ref[...] = level_matrix(mix_ref[1])
    half = (R + 2) // 2
    low = lanes((8, C)) % SLOT < H
    for p in range(half):
        a, b = rl_ref[pl.ds(8 * p, 8), :], rr_ref[pl.ds(8 * p, 8), :]
        side_ref[pl.ds(8 * p, 8), :] = jnp.where(low, a, shift(b, H))
        side_ref[pl.ds(8 * (p + half), 8), :] = jnp.where(low, shift(a, -H), b)
    at = lanes((8, C)) % SLOT
    for ref, first in ((top_ref, 0), (bot_ref, R - H)):
        ref[pl.ds(0, H * K), :] = core_in[pl.ds(first * K, H * K), :]
        for j in range(HALF):
            d, near, far = corner_rows(j, first == 0)
            a, b = (side_ref[pl.ds(8 * (first + i), 8), :] for i in (near, far))
            both = jnp.where(at < d, shift(b, d - H), a)
            both = jnp.where(at >= SLOT - d, shift(b, H - d), both)
            ref[pl.ds(H * K + 8 * j, 8), :] = both
        ref[pl.ds(H * K + 8 * HALF, 2 * R), :] = mk_ref[...]
        ref[pl.ds(H * K + 8 * HALF + 2 * R, 8), :] = side_ref[pl.ds(8 * R, 8), :]


def split(x):
    high = x.astype(jnp.bfloat16)
    return high, (x - high.astype(jnp.float32)).astype(jnp.bfloat16)


def level_matrix(mix):
    high, low = split(mix)
    return jnp.concatenate([high, high, low], axis=1)


def levels(matrix, u):
    high, low = split(u)
    return jnp.dot(
        matrix, jnp.concatenate([high, low, high], axis=0), preferred_element_type=jnp.float32
    )


def coefficients(m, k, scale, by, out_ref):
    moves = (
        lambda a: pltpu.roll(a, 1, 0),
        lambda a: pltpu.roll(a, a.shape[0] - 1, 0),
        lambda a: shift(a, by),
        lambda a: shift(a, -by),
    )
    total = None
    for i, move in enumerate(moves):
        c = (0.5 * scale) * (k + move(k)) * (m * move(m))
        out_ref[i + 1] = c
        total = c if total is None else total + c
    out_ref[0] = m * (1.0 - total)


def fine_coarse_coefficients(mk, first, count, cf_ref, cc_ref):
    wide = lambda i: jnp.concatenate([mk[i], mk[i + 1]], axis=1)
    coefficients(wide(0), wide(2), 1.0, 1, cf_ref)
    at, after = pl.ds(first, count, stride=2), pl.ds(first + 1, count, stride=2)

    def blocks(i):
        return pair_sum(jnp.concatenate([mk[j, at] + mk[j, after] for j in (i, i + 1)], axis=1))

    wet = blocks(0)
    coefficients(
        jnp.minimum(wet, 1.0), 0.25 * blocks(2), 0.75, 2, cc_ref.at[pl.ds(0, 5)]
    )
    cc_ref[5] = 1.0 / jnp.maximum(wet, 1.0)


def stencil(coef_ref, row, by, u, north, south, matrix):
    c = [coef_ref[i, pl.ds(row, 1), :] for i in range(5)]
    near = c[0] * u + c[1] * north + c[2] * south
    side = c[3] * shift(u, by) + c[4] * shift(u, -by)
    return (near + side) + levels(matrix, u)


def step_row(src, r, coef_ref, row, by, matrix):
    return stencil(coef_ref, row, by, src[r], src[r - 1], src[r + 1], matrix)


def restrict(src, i, cc_ref, row):
    return pair_sum(src[1 + 2 * i] + src[2 + 2 * i]) * cc_ref[5, pl.ds(row, 1), :]


def own_kernel(
    slot_ref, core_ref, side_ref, mk_ref, fine_mix, coarse_mix, u0, u1, u2, u3, rs, gs, qs, core_cf, mk, cf, cc
):
    for r in range(R):
        u0[H + r, :, :C] = core_ref[pl.ds(r * K, K), :]
        u0[H + r, :, C:] = unpack_row(side_ref[pl.ds(8 * r, 8), :])
    coefs = unpack_row(side_ref[pl.ds(8 * R, 8), :])
    for i in range(2):
        mk[2 * i] = mk_ref[pl.ds(i * R, R), :]
        mk[2 * i + 1] = coefs[i * R : i * R + R]
    fine_coarse_coefficients(mk, 0, R // 2, cf, cc)
    for margin, src, dst in ((1, u0, u1), (2, u1, u2), (3, u2, u3)):

        @pl.loop(margin, R - margin, unroll=R - 2 * margin)
        def _(r):
            dst[H + r] = step_row(src, H + r, cf, r, 1, fine_mix[...])

    for i in range(4, 12):
        rs[i] = restrict(u0, i, cc, i - 4)
    for i in range(5, 11):
        gs[i] = step_row(rs, i, cc, i - 4, 2, coarse_mix[...])
    for i in range(6, 10):
        qs[i] = restrict(u3, i, cc, i - 4) - jnp.minimum(slot_ref[0], 1.0) * gs[i]
    for i in range(5):
        core_cf[i] = cf[i, :, :C]


PAIRS3 = [(i, i + 1) for i in range(1, 15, 2)]
PAIRS2 = [(2, 13), *PAIRS3[1:6]]
PAIRS1 = PAIRS3[1:6]


def join(qs, pair):
    even = lanes((K, W)) % 2 == 0
    return jnp.where(even, qs[pair[0]], by_tile(lambda t: shift(t, 1), qs[pair[1]]))


def put_q3(qs, out_ref, indices):
    for p in indices:
        both = join(qs, PAIRS3[p])
        out_ref[pl.ds(p * K, K), :] = both[:, :C]
        out_ref[pl.ds(7 * K + 8 * p, 8), :] = pack_row(both[:, C:])


def ends3(q3_ref, p):
    return q3_ref[pl.ds(7 * K + 8 * p, 8), :]


def put_q2(qs, q3_ref, out_ref):
    both = join(qs, PAIRS2[0])
    out_ref[pl.ds(0, K), :] = both[:, :C]
    out_ref[pl.ds(K, 5 * K), :] = q3_ref[pl.ds(K, 5 * K), :]
    ends = [pack_row(both[:, C:])] + [ends3(q3_ref, p) for p in range(1, 6)]
    low = lanes((8, C)) % SLOT < H
    for j in range(3):
        both = jnp.where(low, shift(ends[j], -5), shift(ends[j + 3], 4))
        out_ref[pl.ds(6 * K + 8 * j, 8), :] = both


def put_q1(qs, q3_ref, out_ref):
    for p, core in enumerate((q3_ref[pl.ds(K, K), :], join(qs, (5, 10))[:, :C], q3_ref[pl.ds(5 * K, K), :])):
        out_ref[pl.ds(p * K, K), :] = core
    ends = [ends3(q3_ref, p) for p in range(1, 6)]
    at = lanes((8, C)) % SLOT
    both = shift(ends[3], 5)
    for k in (2, 1, 0):
        both = jnp.where(at < 4 * k + 4, shift(ends[k], 4 * k - 7), both)
    out_ref[pl.ds(3 * K, 8), :] = both
    out_ref[pl.ds(3 * K + 8, 8), :] = ends[4]
    inner = [pack_row(q3_ref[pl.ds(3 * K, K), :]), pack_row(join(qs, (6, 9))[:, :C])]
    out_ref[pl.ds(3 * K + 16, 8), :] = jnp.where(at < H, shift(inner[0], -5), shift(inner[1], 4))


def take_q1(in_ref, inner_ref, a):
    def put(pair, at, value):
        a[pair[0], :, at] = value
        a[pair[1], :, at] = shift(value, -1)

    core, side = pl.ds(0, C), pl.ds(C, C)
    for p, pair in enumerate(PAIRS1):
        packed = in_ref[pl.ds(3 * K + (8 if p == 4 else 0), 8), :]
        put(pair, side, unpack_row(packed if p == 4 else shift(packed, 7 - 4 * p)))
    for p, pair in enumerate(((3, 4), (5, 10), (11, 12))):
        put(pair, core, in_ref[pl.ds(p * K, K), :])
    lane = lanes((K, C))
    inside = (lane >= 4) & (lane < C - 4)
    packed = in_ref[pl.ds(3 * K + 16, 8), :]
    for pair, by in (((7, 8), 5), ((6, 9), -4)):
        ends = unpack_row(shift(packed, by))
        for i, value in zip(pair, (ends, shift(ends, -1))):
            a[i, :, core] = jnp.where(inside, inner_ref[i - 6], value)


def take_q(in_ref, pairs, write):
    for p, (first, second) in enumerate(pairs):
        n = len(pairs)
        ends = lambda j: in_ref[pl.ds(n * K + 8 * j, 8), :]
        packed = ends(p) if n == 7 else shift(ends(p % 3), 5 if p < 3 else -4)
        both = jnp.concatenate([in_ref[pl.ds(p * K, K), :], unpack_row(packed)], axis=1)
        write(first, both)
        write(second, by_tile(lambda t: shift(t, -1), both))


def put_ring(src, out_ref):
    for i, r in enumerate(RING):
        out_ref[pl.ds(Q1 + i * K, K), :] = src[H + r, :, :C]
    at = lanes((8, C)) % SLOT
    for i, r in enumerate(SIDE):
        a, b, c = (pack_row(src[H + r + d, :, :C]) for d in (0, 4, 8))
        both = jnp.where(at < 2 * REACH, shift(a, -2 * REACH), b)
        both = jnp.where(at < 4 * REACH, both, shift(c, 2 * REACH))
        out_ref[pl.ds(Q1 + len(RING) * K + 8 * i, 8), :] = both


def take_ring(in_ref, inner_ref):
    rows = {r: in_ref[pl.ds(Q1 + i * K, K), :] for i, r in enumerate(RING)}
    lane = lanes((K, C))
    inside = (lane >= REACH) & (lane < C - REACH)
    for i, r in enumerate(SIDE):
        packed = in_ref[pl.ds(Q1 + len(RING) * K + 8 * i, 8), :]
        for d, by in ((0, 2 * REACH), (4, 0), (8, -2 * REACH)):
            if r + d not in rows:
                ends = unpack_row(shift(packed, by))
                rows[r + d] = jnp.where(inside, inner_ref[pl.ds((r + d) * K, K), :], ends)
    return [rows[r] for r in range(R)]


def outer_rows(
    upper, slot_ref, mk_ref, side_ref, fine_mix, coarse_mix, halo_ref, states, cc_out, mk, cf, cc
):
    u0, u1, u2, u3, rs, gs, qs = states
    mk[...] = jnp.zeros_like(mk)
    first = 0 if upper else H + R
    for i, ends in enumerate(corner_ends(halo_ref, not upper)):
        u0[first + i, :, :C] = halo_ref[pl.ds(i * K, K), :]
        u0[first + i, :, C:] = jnp.zeros((K, C), jnp.float32) if ends is None else unpack_row(ends)
    at = H * K + 8 * HALF
    for j, ref, at, side, side_at in (
        (0 if upper else 2, halo_ref, at, halo_ref, at + 2 * R),
        (1, mk_ref, 0, side_ref, 8 * R),
    ):
        coefs = unpack_row(side[pl.ds(side_at, 8), :])
        for i in range(2):
            mk[2 * i, pl.ds(j * R, R), :] = ref[pl.ds(at + i * R, R), :]
            mk[2 * i + 1, pl.ds(j * R, R), :] = coefs[i * R : i * R + R]
    fine_coarse_coefficients(mk, R - 8, NC, cf, cc)
    for margin, src, dst in ((1, u0, u1), (2, u1, u2), (3, u2, u3)):

        @pl.loop(0, H, unroll=H)
        def _(i):
            r = margin + i if upper else E - 1 - margin - i
            dst[r] = step_row(src, r, cf, r + BASE, 1, fine_mix[...])

    mirror = lambda rows: rows if upper else [NC - 1 - i for i in rows]
    for i in mirror([0, 1, 2, 3]):
        rs[i] = restrict(u0, i, cc, i)
    for i in mirror([1, 2, 3, 4]):
        gs[i] = step_row(rs, i, cc, i, 2, coarse_mix[...])
    for i in mirror([1, 2, 3, 4, 5]):
        qs[i] = restrict(u3, i, cc, i) - jnp.minimum(slot_ref[0], 1.0) * gs[i]
    half = pl.ds(0 if upper else NC // 2, NC // 2)
    for i in range(6):
        cc_out[i, half, :] = cc[i, half, :]


FIRST_UPPER = False


def first_side_kernel(*refs):
    *ins, mk, cf, cc = refs
    states, cc_out, q3_ref = ins[13:20], ins[20], ins[21]
    outer_rows(FIRST_UPPER, *ins[:6], states, cc_out, mk, cf, cc)
    put_q3(states[6], q3_ref, range(4) if FIRST_UPPER else range(3, 7))


def second_side_kernel(*refs):
    *ins, mk, cf, cc = refs
    states, cc_out, q3_ref, q2_ref = ins[15:22], ins[22], ins[23], ins[24]
    outer_rows(not FIRST_UPPER, *ins[:6], states, cc_out, mk, cf, cc)
    put_q3(states[6], q3_ref, range(4, 7) if FIRST_UPPER else range(3))
    put_q2(states[6], q3_ref, q2_ref)


def near_message_kernel(u3, qs, q3_ref, out_ref):
    put_q1(qs, q3_ref, out_ref)
    put_ring(u3, out_ref)


def before_kernel(
    slot_ref, core_ref, fine_mix, coarse_mix, cf_ref, u3, cc_ref, mk_ref,
    inner_ref, rest_ref, qi_ref, ua, ub, rs, cc,
):
    for r in range(R):
        ua[r] = core_ref[pl.ds(r * K, K), :]
    for i in range(6):
        cc[i] = cc_ref[i, :, :C]
    for i in range(R // 2):
        rs[i] = block_mean((ua[2 * i], ua[2 * i + 1]), cc_ref, i)
    for margin, src, dst in ((1, ua, ub), (2, ub, ua), (3, ua, None)):
        for r in range(margin, R - margin):
            value = step_row(src, r, cf_ref, r, 1, fine_mix[...])
            if dst is None:
                inner_ref[pl.ds(r * K, K), :] = value
            else:
                dst[r] = value
    for r in RING:
        inner_ref[pl.ds(r * K, K), :] = jnp.zeros((K, C), jnp.float32)
    for i in range(2, 6):
        pair = [inner_ref[pl.ds(r * K, K), :] for r in (2 * i, 2 * i + 1)]
        g = step_row(rs, i, cc, 4 + i, 2, coarse_mix[...])
        qi_ref[i - 2] = block_mean(pair, cc_ref, i) - jnp.clip(slot_ref[0] - 1.0, 0.0, 1.0) * g
    for i in range(R // 2):
        pair = [u3[H + r, :, :C] for r in (2 * i, 2 * i + 1)]
        fc = spread(block_mean(pair, cc_ref, i))
        for r, value in zip((2 * i, 2 * i + 1), pair):
            rest_ref[pl.ds(r * K, K), :] = value - mk_ref[pl.ds(r, 1), :] * fc


def block_mean(pair, cc_ref, i):
    total = pair[0] + pair[1]
    return (total + shift(total, -1)) * cc_ref[5, 4 + i : 5 + i, :C]


def near_kernel(q1_ref, inner_ref, qi_ref, cc_ref, mk_ref, _, a, base_ref):
    take_q1(q1_ref, qi_ref, a)
    rows = take_ring(q1_ref, inner_ref)
    for i in range(R // 2):
        pair = rows[2 * i], rows[2 * i + 1]
        fc = spread(block_mean(pair, cc_ref, i))
        for r, value in zip((2 * i, 2 * i + 1), pair):
            base_ref[pl.ds(r * K, K), :] = value - mk_ref[pl.ds(r, 1), :] * fc


def far_kernel(coarse_mix, cc_ref, q3_ref, b, a):
    take_q(q3_ref, PAIRS3, lambda i, value: a.__setitem__(i, value))
    for i in range(2, 14):
        b[i] = step_row(a, i, cc_ref, i, 2, coarse_mix[...])


def last_kernel(
    slot_ref, mk_ref, coarse_mix, cc_ref, x_ref, far, near, q2_ref, qs, rest_ref, base_ref,
    out_hbm, next_hbm, a, b, out_ref, next_ref, sems,
):
    take_q(q2_ref, PAIRS2, lambda i, value: b.__setitem__(i, far[i] + value))
    for i in range(3, 13):
        a[i] = near[i] + step_row(b, i, cc_ref, i, 2, coarse_mix[...])
    first = slot_ref[0] == 0.0

    def put(ref, from_ref, i, value):
        value = spread(value)
        for r in (2 * i, 2 * i + 1):
            total = from_ref[pl.ds(r * K, K), :] + mk_ref[pl.ds(r, 1), :] * value
            ref[pl.ds(r, K, stride=R), :] = total

    @pl.when(first)
    def _():
        next_ref[...] = x_ref[...]

    @pl.when(jnp.logical_not(first))
    def _():
        for i in range(R // 2):
            put(next_ref, base_ref, i, a[4 + i, :, :C])

    next_copy = pltpu.make_async_copy(next_ref, next_hbm, sems.at[0])
    next_copy.start()
    halves = []
    for i in range(R // 2):
        z = qs[4 + i] + step_row(a, 4 + i, cc_ref, 4 + i, 2, coarse_mix[...])
        put(out_ref, rest_ref, i, z[:, :C])
        if i % 4 == 3:
            rows = pl.ds(i // 4 * 8, 8)
            halves.append(
                pltpu.make_async_copy(
                    out_ref.reshape(K, R, C).at[:, rows, :],
                    out_hbm.reshape(K, R, C).at[:, rows, :],
                    sems.at[1 + i // 4],
                )
            )
            halves[-1].start()
    for copy in (next_copy, *halves):
        copy.wait()


def f32(*shape):
    return jax.ShapeDtypeStruct(shape, jnp.float32)


def scratch(*shape):
    return pltpu.VMEM(shape, jnp.float32)


def call(kernel, n_in, outs, scratches=(), smem=0, aliases=None, out_spec=VMEM, cost=None):
    return pl.pallas_call(
        kernel,
        out_shape=outs,
        in_specs=[SMEM] * smem + [VMEM] * (n_in - smem),
        out_specs=jax.tree.map(lambda _: out_spec, outs),
        scratch_shapes=list(scratches),
        input_output_aliases=aliases or {},
        cost_estimate=cost,
        compiler_params=pltpu.CompilerParams(vmem_limit_bytes=40 * 1024 * 1024),
    )


def moved(value, axis, by, wrap=False):
    n = lax.axis_size(axis)
    pairs = [(i, (i + by) % n) for i in range(n) if wrap or 0 <= i + by < n]
    return lax.ppermute(value, axis, pairs)


def body(start, wet, kappa, mixing):
    x = start.reshape(K * R, C)
    slot = lax.axis_index("tm").astype(jnp.float32).reshape(1)
    mixing = mixing[None] * jnp.array([1.0, 3.0], jnp.float32)[:, None, None]
    lon = (R + 2) * 4
    left, right, core, mk = call(
        edge_kernel, 2, (f32(lon, C), f32(lon, C), f32(R * K, C), f32(2 * R, C))
    )(x, jnp.where(wet > 0, kappa, -kappa))
    from_left = moved(left, "lon", 1, True)
    from_right = moved(right, "lon", -1, True)
    matrix = jax.ShapeDtypeStruct((K, 3 * K), jnp.bfloat16)
    core, top, bottom, side, fine_mix, coarse_mix = call(
        halo_kernel,
        5,
        (f32(R * K, C), f32(LAT, C), f32(LAT, C), f32(8 * (R + 2), C), matrix, matrix),
        aliases={0: 0},
    )(core, mk, from_left, from_right, mixing)
    down = moved(top, "lat", -1)
    up = moved(bottom, "lat", 1)
    before = moved(core, "tm", 1)
    fine, coarse = f32(E, K, W), f32(NC, K, W)
    shapes = (fine,) * 4 + (coarse,) * 3
    *states, cf = call(
        own_kernel,
        6,
        shapes + (f32(5, R, C),),
        [scratch(4, R, C), scratch(5, R, W), scratch(6, R // 2, W)],
        smem=1,
    )(slot, core, side, mk, fine_mix, coarse_mix)
    parts = [scratch(4, 48, C), scratch(5, 48, W), scratch(6, NC, W)]
    coefs = f32(6, NC, W)
    states = call(
        first_side_kernel,
        13,
        shapes + (coefs, f32(Q3, C)),
        parts,
        smem=1,
        aliases={6 + i: i for i in range(7)},
    )(slot, mk, side, fine_mix, coarse_mix, up if FIRST_UPPER else down, *states)
    *states, cc, q3, q2 = call(
        second_side_kernel,
        15,
        shapes + (coefs, f32(Q3, C), f32(Q2, C)),
        parts,
        smem=1,
        aliases={6 + i: i for i in range(9)},
    )(slot, mk, side, fine_mix, coarse_mix, down if FIRST_UPPER else up, *states)
    u3, qs = states[3], states[6]
    q1 = call(
        near_message_kernel,
        3,
        f32(Q1 + RG, C),
        cost=pl.CostEstimate(flops=300 * 10**8, bytes_accessed=0, transcendentals=0),
    )(u3, qs, q3)
    q3, q2, q1 = moved(q3, "tm", 3), moved(q2, "tm", 2), moved(q1, "tm", 1)
    inner, rest, inner_q = call(
        before_kernel,
        8,
        (f32(R * K, C), f32(R * K, C), f32(4, K, C)),
        [scratch(R, K, C), scratch(R, K, C), scratch(R // 2, K, C), scratch(6, NC, C)],
        smem=1,
    )(slot, before, fine_mix, coarse_mix, cf, u3, cc, mk)
    far = call(
        far_kernel,
        3,
        coarse,
        [scratch(NC, K, W)],
        cost=pl.CostEstimate(flops=20 * 10**8, bytes_accessed=0, transcendentals=0),
    )(coarse_mix, cc, q3)
    near, base = call(near_kernel, 6, (coarse, f32(R * K, C)))(
        q1, inner, inner_q, cc, mk, far
    )
    out, following = call(
        last_kernel,
        11,
        (f32(K * R, C), f32(K * R, C)),
        [scratch(NC, K, W)] * 2 + [scratch(K * R, C)] * 2 + [pltpu.SemaphoreType.DMA((3,))],
        smem=1,
        out_spec=ANY,
    )(slot, mk, coarse_mix, cc, x, far, near, q2, qs, rest, base)
    return out.reshape(1, K, R, C), following.reshape(1, K, R, C)


def solution(mesh):
    in_specs = (P("tm", None, "lat", "lon"), P("lat", "lon"), P("lat", "lon"), P())
    out_specs = (P("tm", None, "lat", "lon"), P("tm", None, "lat", "lon"))
    return jax.shard_map(body, mesh=mesh, in_specs=in_specs, out_specs=out_specs, check_vma=False)
```

```python
import jax
import jax.numpy as jnp
from jax import lax
from jax.experimental import pallas as pl
from jax.experimental.pallas import tpu as pltpu
from jax.sharding import PartitionSpec as P

K = 48
R = 16
C = 128
H = 9
E = R + 2 * H
W = 2 * C
G = K // 8
SLOT = 2 * H
BASE = R - H
NC = 16
REACH = 3
RING = [*range(REACH), *range(R - REACH, R)]
SIDE = range(2, 6)
Q3, Q2, Q1, RG = 49 * 8, 39 * 8, 21 * 8, 40 * 8
HALF = (H - 1) // 2
LAT = H * K + 8 * HALF + 2 * R + 8
VMEM = pl.BlockSpec(memory_space=pltpu.VMEM)
SMEM = pl.BlockSpec(memory_space=pltpu.SMEM)
ANY = pl.BlockSpec(memory_space=pl.ANY)


def lanes(shape):
    return lax.broadcasted_iota(jnp.int32, shape, len(shape) - 1)


def shift(x, by):
    return pltpu.roll(x, by % x.shape[-1], x.ndim - 1)


def by_tile(fn, x):
    return jnp.concatenate([fn(x[:, :C]), fn(x[:, C:])], axis=1)


def pair_sum(x):
    return x + by_tile(lambda t: shift(t, -1), x)


def spread(x):
    return jnp.where(lanes(x.shape) % 2 == 0, x, shift(x, 1))


def pack_row(row):
    lane = lanes((8, C))
    out = shift(row[0:8], H)
    for g in range(1, G):
        out = jnp.where(lane < SLOT * g, out, shift(row[8 * g : 8 * g + 8], SLOT * g + H))
    return out


def unpack_row(packed):
    return jnp.concatenate([shift(packed, C - H - SLOT * g) for g in range(G)], axis=0)


def edge_kernel(x_ref, signed_ref, left_ref, right_ref, core_ref, mk_ref):
    signed = signed_ref[...]
    mask = jnp.where(signed > 0.0, 1.0, 0.0)
    mk_ref[pl.ds(0, R), :] = mask
    mk_ref[pl.ds(R, R), :] = jnp.abs(signed)
    rows = []
    for r in range(R):
        row = x_ref[pl.ds(r, K, stride=R), :] * mask[r : r + 1]
        core_ref[pl.ds(r * K, K), :] = row
        rows.append(pack_row(row))
    coefs = pack_row(jnp.concatenate([mk_ref[...], jnp.zeros((R, C), jnp.float32)], axis=0))
    rows += [coefs, coefs]
    half = len(rows) // 2
    low = lanes((8, C)) % SLOT < H
    for p in range(half):
        a, b = rows[p], rows[p + half]
        left_ref[pl.ds(8 * p, 8), :] = jnp.where(low, a, shift(b, H))
        right_ref[pl.ds(8 * p, 8), :] = jnp.where(low, shift(a, -H), b)


def corner_rows(j, first_rows):
    d = j + 1
    place = (lambda k: k - 1) if first_rows else (lambda k: H - k)
    return d, place(d), place(H - d)


def corner_ends(halo_ref, first_rows):
    low = lanes((8, C)) % SLOT < H
    ends = [None] * H
    for j in range(HALF):
        d, near, far = corner_rows(j, first_rows)
        both = halo_ref[pl.ds(H * K + 8 * j, 8), :]
        ends[near] = both
        ends[far] = jnp.where(low, shift(both, H - d), shift(both, d - H))
    return ends


def halo_kernel(
    core_in, mk_ref, rl_ref, rr_ref, mix_ref,
    core_ref, top_ref, bot_ref, side_ref, fine_ref, coarse_ref,
):
    fine_ref[...] = level_matrix(mix_ref[0])
    coarse_ref[...] = level_matrix(mix_ref[1])
    half = (R + 2) // 2
    low = lanes((8, C)) % SLOT < H
    for p in range(half):
        a, b = rl_ref[pl.ds(8 * p, 8), :], rr_ref[pl.ds(8 * p, 8), :]
        side_ref[pl.ds(8 * p, 8), :] = jnp.where(low, a, shift(b, H))
        side_ref[pl.ds(8 * (p + half), 8), :] = jnp.where(low, shift(a, -H), b)
    at = lanes((8, C)) % SLOT
    for ref, first in ((top_ref, 0), (bot_ref, R - H)):
        ref[pl.ds(0, H * K), :] = core_in[pl.ds(first * K, H * K), :]
        for j in range(HALF):
            d, near, far = corner_rows(j, first == 0)
            a, b = (side_ref[pl.ds(8 * (first + i), 8), :] for i in (near, far))
            both = jnp.where(at < d, shift(b, d - H), a)
            both = jnp.where(at >= SLOT - d, shift(b, H - d), both)
            ref[pl.ds(H * K + 8 * j, 8), :] = both
        ref[pl.ds(H * K + 8 * HALF, 2 * R), :] = mk_ref[...]
        ref[pl.ds(H * K + 8 * HALF + 2 * R, 8), :] = side_ref[pl.ds(8 * R, 8), :]


def split(x):
    high = x.astype(jnp.bfloat16)
    return high, (x - high.astype(jnp.float32)).astype(jnp.bfloat16)


def level_matrix(mix):
    high, low = split(mix)
    return jnp.concatenate([high, high, low], axis=1)


def levels(matrix, u):
    high, low = split(u)
    return jnp.dot(
        matrix, jnp.concatenate([high, low, high], axis=0), preferred_element_type=jnp.float32
    )


def coefficients(m, k, scale, by, out_ref):
    moves = (
        lambda a: pltpu.roll(a, 1, 0),
        lambda a: pltpu.roll(a, a.shape[0] - 1, 0),
        lambda a: shift(a, by),
        lambda a: shift(a, -by),
    )
    total = None
    for i, move in enumerate(moves):
        c = (0.5 * scale) * (k + move(k)) * (m * move(m))
        out_ref[i + 1] = c
        total = c if total is None else total + c
    out_ref[0] = m * (1.0 - total)


def fine_coarse_coefficients(mk, first, count, cf_ref, cc_ref):
    wide = lambda i: jnp.concatenate([mk[i], mk[i + 1]], axis=1)
    coefficients(wide(0), wide(2), 1.0, 1, cf_ref)
    at, after = pl.ds(first, count, stride=2), pl.ds(first + 1, count, stride=2)

    def blocks(i):
        return pair_sum(jnp.concatenate([mk[j, at] + mk[j, after] for j in (i, i + 1)], axis=1))

    wet = blocks(0)
    coefficients(
        jnp.minimum(wet, 1.0), 0.25 * blocks(2), 0.75, 2, cc_ref.at[pl.ds(0, 5)]
    )
    cc_ref[5] = 1.0 / jnp.maximum(wet, 1.0)


def stencil(coef_ref, row, by, u, north, south, matrix):
    c = [coef_ref[i, pl.ds(row, 1), :] for i in range(5)]
    near = c[0] * u + c[1] * north + c[2] * south
    side = c[3] * shift(u, by) + c[4] * shift(u, -by)
    return (near + side) + levels(matrix, u)


def step_row(src, r, coef_ref, row, by, matrix):
    return stencil(coef_ref, row, by, src[r], src[r - 1], src[r + 1], matrix)


def restrict(src, i, cc_ref, row):
    return pair_sum(src[1 + 2 * i] + src[2 + 2 * i]) * cc_ref[5, pl.ds(row, 1), :]


def own_kernel(
    slot_ref, core_ref, side_ref, mk_ref, fine_mix, coarse_mix, u0, u1, u2, u3, rs, gs, qs, core_cf, mk, cf, cc
):
    for r in range(R):
        u0[H + r, :, :C] = core_ref[pl.ds(r * K, K), :]
        u0[H + r, :, C:] = unpack_row(side_ref[pl.ds(8 * r, 8), :])
    coefs = unpack_row(side_ref[pl.ds(8 * R, 8), :])
    for i in range(2):
        mk[2 * i] = mk_ref[pl.ds(i * R, R), :]
        mk[2 * i + 1] = coefs[i * R : i * R + R]
    fine_coarse_coefficients(mk, 0, R // 2, cf, cc)
    for margin, src, dst in ((1, u0, u1), (2, u1, u2), (3, u2, u3)):

        @pl.loop(margin, R - margin, unroll=R - 2 * margin)
        def _(r):
            dst[H + r] = step_row(src, H + r, cf, r, 1, fine_mix[...])

    @pl.when(slot_ref[0] == 0.0)
    def _():
        for i in range(6, 10):
            qs[i] = restrict(u3, i, cc, i - 4)

    @pl.when(slot_ref[0] > 0.0)
    def _():
        for i in range(4, 12):
            rs[i] = restrict(u0, i, cc, i - 4)
        for i in range(5, 11):
            gs[i] = step_row(rs, i, cc, i - 4, 2, coarse_mix[...])
        for i in range(6, 10):
            qs[i] = restrict(u3, i, cc, i - 4) - gs[i]

    for i in range(5):
        core_cf[i] = cf[i, :, :C]


PAIRS3 = [(i, i + 1) for i in range(1, 15, 2)]
PAIRS2 = [(2, 13), *PAIRS3[1:6]]
PAIRS1 = PAIRS3[1:6]


def join(qs, pair):
    even = lanes((K, W)) % 2 == 0
    return jnp.where(even, qs[pair[0]], by_tile(lambda t: shift(t, 1), qs[pair[1]]))


def put_q3(qs, out_ref, indices):
    for p in indices:
        both = join(qs, PAIRS3[p])
        out_ref[pl.ds(p * K, K), :] = both[:, :C]
        out_ref[pl.ds(7 * K + 8 * p, 8), :] = pack_row(both[:, C:])


def ends3(q3_ref, p):
    return q3_ref[pl.ds(7 * K + 8 * p, 8), :]


def put_q2(qs, q3_ref, out_ref):
    both = join(qs, PAIRS2[0])
    out_ref[pl.ds(0, K), :] = both[:, :C]
    out_ref[pl.ds(K, 5 * K), :] = q3_ref[pl.ds(K, 5 * K), :]
    ends = [pack_row(both[:, C:])] + [ends3(q3_ref, p) for p in range(1, 6)]
    low = lanes((8, C)) % SLOT < H
    for j in range(3):
        both = jnp.where(low, shift(ends[j], -5), shift(ends[j + 3], 4))
        out_ref[pl.ds(6 * K + 8 * j, 8), :] = both


def put_q1(qs, q3_ref, out_ref):
    for p, core in enumerate((q3_ref[pl.ds(K, K), :], join(qs, (5, 10))[:, :C], q3_ref[pl.ds(5 * K, K), :])):
        out_ref[pl.ds(p * K, K), :] = core
    ends = [ends3(q3_ref, p) for p in range(1, 6)]
    at = lanes((8, C)) % SLOT
    both = shift(ends[3], 5)
    for k in (2, 1, 0):
        both = jnp.where(at < 4 * k + 4, shift(ends[k], 4 * k - 7), both)
    out_ref[pl.ds(3 * K, 8), :] = both
    out_ref[pl.ds(3 * K + 8, 8), :] = ends[4]
    inner = [pack_row(q3_ref[pl.ds(3 * K, K), :]), pack_row(join(qs, (6, 9))[:, :C])]
    out_ref[pl.ds(3 * K + 16, 8), :] = jnp.where(at < H, shift(inner[0], -5), shift(inner[1], 4))


def take_q1(in_ref, inner_ref, a):
    def put(pair, at, value):
        a[pair[0], :, at] = value
        a[pair[1], :, at] = shift(value, -1)

    core, side = pl.ds(0, C), pl.ds(C, C)
    for p, pair in enumerate(PAIRS1):
        packed = in_ref[pl.ds(3 * K + (8 if p == 4 else 0), 8), :]
        put(pair, side, unpack_row(packed if p == 4 else shift(packed, 7 - 4 * p)))
    for p, pair in enumerate(((3, 4), (5, 10), (11, 12))):
        put(pair, core, in_ref[pl.ds(p * K, K), :])
    lane = lanes((K, C))
    inside = (lane >= 4) & (lane < C - 4)
    packed = in_ref[pl.ds(3 * K + 16, 8), :]
    for pair, by in (((7, 8), 5), ((6, 9), -4)):
        ends = unpack_row(shift(packed, by))
        for i, value in zip(pair, (ends, shift(ends, -1))):
            a[i, :, core] = jnp.where(inside, inner_ref[i - 6], value)


def take_q(in_ref, pairs, write):
    for p, (first, second) in enumerate(pairs):
        n = len(pairs)
        ends = lambda j: in_ref[pl.ds(n * K + 8 * j, 8), :]
        packed = ends(p) if n == 7 else shift(ends(p % 3), 5 if p < 3 else -4)
        both = jnp.concatenate([in_ref[pl.ds(p * K, K), :], unpack_row(packed)], axis=1)
        write(first, both)
        write(second, by_tile(lambda t: shift(t, -1), both))


def put_ring(src, out_ref):
    for i, r in enumerate(RING):
        out_ref[pl.ds(Q1 + i * K, K), :] = src[H + r, :, :C]
    at = lanes((8, C)) % SLOT
    for i, r in enumerate(SIDE):
        a, b, c = (pack_row(src[H + r + d, :, :C]) for d in (0, 4, 8))
        both = jnp.where(at < 2 * REACH, shift(a, -2 * REACH), b)
        both = jnp.where(at < 4 * REACH, both, shift(c, 2 * REACH))
        out_ref[pl.ds(Q1 + len(RING) * K + 8 * i, 8), :] = both


def take_ring(in_ref, inner_ref):
    rows = {r: in_ref[pl.ds(Q1 + i * K, K), :] for i, r in enumerate(RING)}
    lane = lanes((K, C))
    inside = (lane >= REACH) & (lane < C - REACH)
    for i, r in enumerate(SIDE):
        packed = in_ref[pl.ds(Q1 + len(RING) * K + 8 * i, 8), :]
        for d, by in ((0, 2 * REACH), (4, 0), (8, -2 * REACH)):
            if r + d not in rows:
                ends = unpack_row(shift(packed, by))
                rows[r + d] = jnp.where(inside, inner_ref[pl.ds((r + d) * K, K), :], ends)
    return [rows[r] for r in range(R)]


def outer_rows(
    upper, slot_ref, mk_ref, side_ref, fine_mix, coarse_mix, halo_ref, states, cc_out, mk, cf, cc
):
    u0, u1, u2, u3, rs, gs, qs = states
    mk[...] = jnp.zeros_like(mk)
    first = 0 if upper else H + R
    for i, ends in enumerate(corner_ends(halo_ref, not upper)):
        u0[first + i, :, :C] = halo_ref[pl.ds(i * K, K), :]
        u0[first + i, :, C:] = jnp.zeros((K, C), jnp.float32) if ends is None else unpack_row(ends)
    at = H * K + 8 * HALF
    for j, ref, at, side, side_at in (
        (0 if upper else 2, halo_ref, at, halo_ref, at + 2 * R),
        (1, mk_ref, 0, side_ref, 8 * R),
    ):
        coefs = unpack_row(side[pl.ds(side_at, 8), :])
        for i in range(2):
            mk[2 * i, pl.ds(j * R, R), :] = ref[pl.ds(at + i * R, R), :]
            mk[2 * i + 1, pl.ds(j * R, R), :] = coefs[i * R : i * R + R]
    fine_coarse_coefficients(mk, R - 8, NC, cf, cc)
    mirror = lambda rows: rows if upper else [NC - 1 - i for i in rows]

    def rows_of(steps, wide, narrow, lowered):
        for margin, src, dst in ((1, u0, u1), (2, u1, u2), (3, u2, u3)):

            @pl.loop(*steps, unroll=steps[1] - steps[0])
            def _(i):
                r = margin + i if upper else E - 1 - margin - i
                dst[r] = step_row(src, r, cf, r + BASE, 1, fine_mix[...])

        for i in mirror(wide):
            rs[i] = restrict(u0, i, cc, i)
        for i in mirror(narrow):
            gs[i] = step_row(rs, i, cc, i, 2, coarse_mix[...])
        for i in mirror(lowered):
            fc = restrict(u3, i, cc, i)
            qs[i] = fc - gs[i] if narrow else fc

    for k in range(4):

        @pl.when(slot_ref[0] == float(k))
        def _():
            wide, narrow = ([*range(k - 1, 4)], [*range(k, 4)]) if k else ([], [])
            rows_of((2 * k, H), wide, [i + 1 for i in narrow], [*range(k + 1, 6)])

    half = pl.ds(0 if upper else NC // 2, NC // 2)
    for i in range(6):
        cc_out[i, half, :] = cc[i, half, :]


FIRST_UPPER = False


def first_side_kernel(*refs):
    *ins, mk, cf, cc = refs
    states, cc_out, q3_ref = ins[13:20], ins[20], ins[21]
    outer_rows(FIRST_UPPER, *ins[:6], states, cc_out, mk, cf, cc)
    put_q3(states[6], q3_ref, range(4) if FIRST_UPPER else range(3, 7))


def second_side_kernel(*refs):
    *ins, mk, cf, cc = refs
    states, cc_out, q3_ref, q2_ref = ins[15:22], ins[22], ins[23], ins[24]
    outer_rows(not FIRST_UPPER, *ins[:6], states, cc_out, mk, cf, cc)
    put_q3(states[6], q3_ref, range(4, 7) if FIRST_UPPER else range(3))
    put_q2(states[6], q3_ref, q2_ref)


def near_message_kernel(u3, qs, q3_ref, out_ref):
    put_q1(qs, q3_ref, out_ref)
    put_ring(u3, out_ref)


def before_kernel(
    slot_ref, core_ref, fine_mix, coarse_mix, cf_ref, u3, cc_ref, mk_ref,
    inner_ref, rest_ref, qi_ref, ua, ub, rs, cc,
):
    for r in range(R):
        ua[r] = core_ref[pl.ds(r * K, K), :]
    for i in range(6):
        cc[i] = cc_ref[i, :, :C]
    for i in range(R // 2):
        rs[i] = block_mean((ua[2 * i], ua[2 * i + 1]), cc_ref, i)
    for margin, src, dst in ((1, ua, ub), (2, ub, ua), (3, ua, None)):
        for r in range(margin, R - margin):
            value = step_row(src, r, cf_ref, r, 1, fine_mix[...])
            if dst is None:
                inner_ref[pl.ds(r * K, K), :] = value
            else:
                dst[r] = value
    for r in RING:
        inner_ref[pl.ds(r * K, K), :] = jnp.zeros((K, C), jnp.float32)
    for i in range(2, 6):
        pair = [inner_ref[pl.ds(r * K, K), :] for r in (2 * i, 2 * i + 1)]
        g = step_row(rs, i, cc, 4 + i, 2, coarse_mix[...])
        qi_ref[i - 2] = block_mean(pair, cc_ref, i) - jnp.clip(slot_ref[0] - 1.0, 0.0, 1.0) * g
    for i in range(R // 2):
        pair = [u3[H + r, :, :C] for r in (2 * i, 2 * i + 1)]
        fc = spread(block_mean(pair, cc_ref, i))
        for r, value in zip((2 * i, 2 * i + 1), pair):
            rest_ref[pl.ds(r * K, K), :] = value - mk_ref[pl.ds(r, 1), :] * fc


def block_mean(pair, cc_ref, i):
    total = pair[0] + pair[1]
    return (total + shift(total, -1)) * cc_ref[5, 4 + i : 5 + i, :C]


def near_kernel(q1_ref, inner_ref, qi_ref, cc_ref, mk_ref, _, a, base_ref):
    take_q1(q1_ref, qi_ref, a)
    rows = take_ring(q1_ref, inner_ref)
    for i in range(R // 2):
        pair = rows[2 * i], rows[2 * i + 1]
        fc = spread(block_mean(pair, cc_ref, i))
        for r, value in zip((2 * i, 2 * i + 1), pair):
            base_ref[pl.ds(r * K, K), :] = value - mk_ref[pl.ds(r, 1), :] * fc


def far_kernel(coarse_mix, cc_ref, q3_ref, b, a):
    take_q(q3_ref, PAIRS3, lambda i, value: a.__setitem__(i, value))
    for i in range(2, 14):
        b[i] = step_row(a, i, cc_ref, i, 2, coarse_mix[...])


def last_kernel(
    slot_ref, mk_ref, coarse_mix, cc_ref, x_ref, far, near, q2_ref, qs, rest_ref, base_ref,
    out_hbm, next_hbm, a, b, out_ref, next_ref, sems,
):
    take_q(q2_ref, PAIRS2, lambda i, value: b.__setitem__(i, far[i] + value))
    for i in range(3, 13):
        a[i] = near[i] + step_row(b, i, cc_ref, i, 2, coarse_mix[...])
    first = slot_ref[0] == 0.0

    def put(ref, from_ref, i, value):
        value = spread(value)
        for r in (2 * i, 2 * i + 1):
            total = from_ref[pl.ds(r * K, K), :] + mk_ref[pl.ds(r, 1), :] * value
            ref[pl.ds(r, K, stride=R), :] = total

    @pl.when(first)
    def _():
        next_ref[...] = x_ref[...]

    @pl.when(jnp.logical_not(first))
    def _():
        for i in range(R // 2):
            put(next_ref, base_ref, i, a[4 + i, :, :C])

    next_copy = pltpu.make_async_copy(next_ref, next_hbm, sems.at[0])
    next_copy.start()
    halves = []
    for i in range(R // 2):
        z = qs[4 + i] + step_row(a, 4 + i, cc_ref, 4 + i, 2, coarse_mix[...])
        put(out_ref, rest_ref, i, z[:, :C])
        if i % 4 == 3:
            rows = pl.ds(i // 4 * 8, 8)
            halves.append(
                pltpu.make_async_copy(
                    out_ref.reshape(K, R, C).at[:, rows, :],
                    out_hbm.reshape(K, R, C).at[:, rows, :],
                    sems.at[1 + i // 4],
                )
            )
            halves[-1].start()
    for copy in (next_copy, *halves):
        copy.wait()


def f32(*shape):
    return jax.ShapeDtypeStruct(shape, jnp.float32)


def scratch(*shape):
    return pltpu.VMEM(shape, jnp.float32)


def call(kernel, n_in, outs, scratches=(), smem=0, aliases=None, out_spec=VMEM, cost=None):
    return pl.pallas_call(
        kernel,
        out_shape=outs,
        in_specs=[SMEM] * smem + [VMEM] * (n_in - smem),
        out_specs=jax.tree.map(lambda _: out_spec, outs),
        scratch_shapes=list(scratches),
        input_output_aliases=aliases or {},
        cost_estimate=cost,
        compiler_params=pltpu.CompilerParams(vmem_limit_bytes=40 * 1024 * 1024),
    )


def moved(value, axis, by, wrap=False):
    n = lax.axis_size(axis)
    pairs = [(i, (i + by) % n) for i in range(n) if wrap or 0 <= i + by < n]
    return lax.ppermute(value, axis, pairs)


def body(start, wet, kappa, mixing):
    x = start.reshape(K * R, C)
    slot = lax.axis_index("tm").astype(jnp.float32).reshape(1)
    mixing = mixing[None] * jnp.array([1.0, 3.0], jnp.float32)[:, None, None]
    lon = (R + 2) * 4
    left, right, core, mk = call(
        edge_kernel, 2, (f32(lon, C), f32(lon, C), f32(R * K, C), f32(2 * R, C))
    )(x, jnp.where(wet > 0, kappa, -kappa))
    from_left = moved(left, "lon", 1, True)
    from_right = moved(right, "lon", -1, True)
    matrix = jax.ShapeDtypeStruct((K, 3 * K), jnp.bfloat16)
    core, top, bottom, side, fine_mix, coarse_mix = call(
        halo_kernel,
        5,
        (f32(R * K, C), f32(LAT, C), f32(LAT, C), f32(8 * (R + 2), C), matrix, matrix),
        aliases={0: 0},
    )(core, mk, from_left, from_right, mixing)
    down = moved(top, "lat", -1)
    up = moved(bottom, "lat", 1)
    before = moved(core, "tm", 1)
    fine, coarse = f32(E, K, W), f32(NC, K, W)
    shapes = (fine,) * 4 + (coarse,) * 3
    *states, cf = call(
        own_kernel,
        6,
        shapes + (f32(5, R, C),),
        [scratch(4, R, C), scratch(5, R, W), scratch(6, R // 2, W)],
        smem=1,
    )(slot, core, side, mk, fine_mix, coarse_mix)
    parts = [scratch(4, 48, C), scratch(5, 48, W), scratch(6, NC, W)]
    coefs = f32(6, NC, W)
    states = call(
        first_side_kernel,
        13,
        shapes + (coefs, f32(Q3, C)),
        parts,
        smem=1,
        aliases={6 + i: i for i in range(7)},
    )(slot, mk, side, fine_mix, coarse_mix, up if FIRST_UPPER else down, *states)
    *states, cc, q3, q2 = call(
        second_side_kernel,
        15,
        shapes + (coefs, f32(Q3, C), f32(Q2, C)),
        parts,
        smem=1,
        aliases={6 + i: i for i in range(9)},
    )(slot, mk, side, fine_mix, coarse_mix, down if FIRST_UPPER else up, *states)
    u3, qs = states[3], states[6]
    q1 = call(
        near_message_kernel,
        3,
        f32(Q1 + RG, C),
        cost=pl.CostEstimate(flops=300 * 10**8, bytes_accessed=0, transcendentals=0),
    )(u3, qs, q3)
    q3, q2, q1 = moved(q3, "tm", 3), moved(q2, "tm", 2), moved(q1, "tm", 1)
    inner, rest, inner_q = call(
        before_kernel,
        8,
        (f32(R * K, C), f32(R * K, C), f32(4, K, C)),
        [scratch(R, K, C), scratch(R, K, C), scratch(R // 2, K, C), scratch(6, NC, C)],
        smem=1,
    )(slot, before, fine_mix, coarse_mix, cf, u3, cc, mk)
    far = call(
        far_kernel,
        3,
        coarse,
        [scratch(NC, K, W)],
        cost=pl.CostEstimate(flops=20 * 10**8, bytes_accessed=0, transcendentals=0),
    )(coarse_mix, cc, q3)
    near, base = call(near_kernel, 6, (coarse, f32(R * K, C)))(
        q1, inner, inner_q, cc, mk, far
    )
    out, following = call(
        last_kernel,
        11,
        (f32(K * R, C), f32(K * R, C)),
        [scratch(NC, K, W)] * 2 + [scratch(K * R, C)] * 2 + [pltpu.SemaphoreType.DMA((3,))],
        smem=1,
        out_spec=ANY,
    )(slot, mk, coarse_mix, cc, x, far, near, q2, qs, rest, base)
    return out.reshape(1, K, R, C), following.reshape(1, K, R, C)


def solution(mesh):
    in_specs = (P("tm", None, "lat", "lon"), P("lat", "lon"), P("lat", "lon"), P())
    out_specs = (P("tm", None, "lat", "lon"), P("tm", None, "lat", "lon"))
    return jax.shard_map(body, mesh=mesh, in_specs=in_specs, out_specs=out_specs, check_vma=False)
```

```python
import jax
import jax.numpy as jnp
from jax import lax
from jax.experimental import pallas as pl
from jax.experimental.pallas import tpu as pltpu
from jax.sharding import PartitionSpec as P

K = 48
R = 16
C = 128
H = 9
E = R + 2 * H
W = 2 * C
G = K // 8
SLOT = 2 * H
BASE = R - H
NC = 16
REACH = 3
RING = [*range(REACH), *range(R - REACH, R)]
SIDE = range(2, 6)
Q3, Q2, Q1, RG = 49 * 8, 39 * 8, 21 * 8, 40 * 8
HALF = (H - 1) // 2
LAT = H * K + 8 * HALF + 2 * R + 8
VMEM = pl.BlockSpec(memory_space=pltpu.VMEM)
SMEM = pl.BlockSpec(memory_space=pltpu.SMEM)
ANY = pl.BlockSpec(memory_space=pl.ANY)


def lanes(shape):
    return lax.broadcasted_iota(jnp.int32, shape, len(shape) - 1)


def shift(x, by):
    return pltpu.roll(x, by % x.shape[-1], x.ndim - 1)


def by_tile(fn, x):
    return jnp.concatenate([fn(x[:, :C]), fn(x[:, C:])], axis=1)


def pair_sum(x):
    return x + by_tile(lambda t: shift(t, -1), x)


def spread(x):
    return jnp.where(lanes(x.shape) % 2 == 0, x, shift(x, 1))


def pack_row(row):
    lane = lanes((8, C))
    out = shift(row[0:8], H)
    for g in range(1, G):
        out = jnp.where(lane < SLOT * g, out, shift(row[8 * g : 8 * g + 8], SLOT * g + H))
    return out


def unpack_row(packed):
    return jnp.concatenate([shift(packed, C - H - SLOT * g) for g in range(G)], axis=0)


def edge_kernel(x_ref, signed_ref, left_ref, right_ref, core_ref, mk_ref):
    signed = signed_ref[...]
    mask = jnp.where(signed > 0.0, 1.0, 0.0)
    mk_ref[pl.ds(0, R), :] = mask
    mk_ref[pl.ds(R, R), :] = jnp.abs(signed)
    rows = []
    for r in range(R):
        row = x_ref[pl.ds(r, K, stride=R), :] * mask[r : r + 1]
        core_ref[pl.ds(r * K, K), :] = row
        rows.append(pack_row(row))
    coefs = pack_row(jnp.concatenate([mk_ref[...], jnp.zeros((R, C), jnp.float32)], axis=0))
    rows += [coefs, coefs]
    half = len(rows) // 2
    low = lanes((8, C)) % SLOT < H
    for p in range(half):
        a, b = rows[p], rows[p + half]
        left_ref[pl.ds(8 * p, 8), :] = jnp.where(low, a, shift(b, H))
        right_ref[pl.ds(8 * p, 8), :] = jnp.where(low, shift(a, -H), b)


def corner_rows(j, first_rows):
    d = j + 1
    place = (lambda k: k - 1) if first_rows else (lambda k: H - k)
    return d, place(d), place(H - d)


def corner_ends(halo_ref, first_rows):
    low = lanes((8, C)) % SLOT < H
    ends = [None] * H
    for j in range(HALF):
        d, near, far = corner_rows(j, first_rows)
        both = halo_ref[pl.ds(H * K + 8 * j, 8), :]
        ends[near] = both
        ends[far] = jnp.where(low, shift(both, H - d), shift(both, d - H))
    return ends


def halo_kernel(
    core_in, mk_ref, rl_ref, rr_ref, mix_ref,
    core_ref, top_ref, bot_ref, side_ref, fine_ref, coarse_ref,
):
    fine_ref[...] = level_matrix(mix_ref[0])
    coarse_ref[...] = level_matrix(mix_ref[1])
    half = (R + 2) // 2
    low = lanes((8, C)) % SLOT < H
    for p in range(half):
        a, b = rl_ref[pl.ds(8 * p, 8), :], rr_ref[pl.ds(8 * p, 8), :]
        side_ref[pl.ds(8 * p, 8), :] = jnp.where(low, a, shift(b, H))
        side_ref[pl.ds(8 * (p + half), 8), :] = jnp.where(low, shift(a, -H), b)
    at = lanes((8, C)) % SLOT
    for ref, first in ((top_ref, 0), (bot_ref, R - H)):
        ref[pl.ds(0, H * K), :] = core_in[pl.ds(first * K, H * K), :]
        for j in range(HALF):
            d, near, far = corner_rows(j, first == 0)
            a, b = (side_ref[pl.ds(8 * (first + i), 8), :] for i in (near, far))
            both = jnp.where(at < d, shift(b, d - H), a)
            both = jnp.where(at >= SLOT - d, shift(b, H - d), both)
            ref[pl.ds(H * K + 8 * j, 8), :] = both
        ref[pl.ds(H * K + 8 * HALF, 2 * R), :] = mk_ref[...]
        ref[pl.ds(H * K + 8 * HALF + 2 * R, 8), :] = side_ref[pl.ds(8 * R, 8), :]


def split(x):
    high = x.astype(jnp.bfloat16)
    return high, (x - high.astype(jnp.float32)).astype(jnp.bfloat16)


def level_matrix(mix):
    high, low = split(mix)
    return jnp.concatenate([high, high, low], axis=1)


def levels(matrix, u):
    high, low = split(u)
    return jnp.dot(
        matrix, jnp.concatenate([high, low, high], axis=0), preferred_element_type=jnp.float32
    )


def coefficients(m, k, scale, by, out_ref):
    moves = (
        lambda a: pltpu.roll(a, 1, 0),
        lambda a: pltpu.roll(a, a.shape[0] - 1, 0),
        lambda a: shift(a, by),
        lambda a: shift(a, -by),
    )
    total = None
    for i, move in enumerate(moves):
        c = (0.5 * scale) * (k + move(k)) * (m * move(m))
        out_ref[i + 1] = c
        total = c if total is None else total + c
    out_ref[0] = m * (1.0 - total)


def fine_coarse_coefficients(mk, first, count, cf_ref, cc_ref):
    wide = lambda i: jnp.concatenate([mk[i], mk[i + 1]], axis=1)
    coefficients(wide(0), wide(2), 1.0, 1, cf_ref)
    at, after = pl.ds(first, count, stride=2), pl.ds(first + 1, count, stride=2)

    def blocks(i):
        return pair_sum(jnp.concatenate([mk[j, at] + mk[j, after] for j in (i, i + 1)], axis=1))

    wet = blocks(0)
    coefficients(
        jnp.minimum(wet, 1.0), 0.25 * blocks(2), 0.75, 2, cc_ref.at[pl.ds(0, 5)]
    )
    cc_ref[5] = 1.0 / jnp.maximum(wet, 1.0)


def stencil(coef_ref, row, by, u, north, south, matrix):
    c = [coef_ref[i, pl.ds(row, 1), :] for i in range(5)]
    near = c[0] * u + c[1] * north + c[2] * south
    side = c[3] * shift(u, by) + c[4] * shift(u, -by)
    return (near + side) + levels(matrix, u)


def step_row(src, r, coef_ref, row, by, matrix):
    return stencil(coef_ref, row, by, src[r], src[r - 1], src[r + 1], matrix)


def restrict(src, i, cc_ref, row):
    return pair_sum(src[1 + 2 * i] + src[2 + 2 * i]) * cc_ref[5, pl.ds(row, 1), :]


def own_kernel(
    slot_ref, core_ref, side_ref, mk_ref, fine_mix, coarse_mix, u0, u1, u2, u3, rs, gs, qs, core_cf, mk, cf, cc
):
    for r in range(R):
        u0[H + r, :, :C] = core_ref[pl.ds(r * K, K), :]
        u0[H + r, :, C:] = unpack_row(side_ref[pl.ds(8 * r, 8), :])
    coefs = unpack_row(side_ref[pl.ds(8 * R, 8), :])
    for i in range(2):
        mk[2 * i] = mk_ref[pl.ds(i * R, R), :]
        mk[2 * i + 1] = coefs[i * R : i * R + R]
    fine_coarse_coefficients(mk, 0, R // 2, cf, cc)
    for margin, src, dst in ((1, u0, u1), (2, u1, u2), (3, u2, u3)):

        @pl.loop(margin, R - margin, unroll=R - 2 * margin)
        def _(r):
            dst[H + r] = step_row(src, H + r, cf, r, 1, fine_mix[...])

    @pl.when(slot_ref[0] == 0.0)
    def _():
        for i in range(6, 10):
            qs[i] = restrict(u3, i, cc, i - 4)

    @pl.when(slot_ref[0] > 0.0)
    def _():
        for i in range(4, 12):
            rs[i] = restrict(u0, i, cc, i - 4)
        for i in range(5, 11):
            gs[i] = step_row(rs, i, cc, i - 4, 2, coarse_mix[...])
        for i in range(6, 10):
            qs[i] = restrict(u3, i, cc, i - 4) - gs[i]

    for i in range(5):
        core_cf[i] = cf[i, :, :C]


PAIRS3 = [(i, i + 1) for i in range(1, 15, 2)]
PAIRS2 = [(2, 13), *PAIRS3[1:6]]
PAIRS1 = PAIRS3[1:6]


def join(qs, pair):
    even = lanes((K, W)) % 2 == 0
    return jnp.where(even, qs[pair[0]], by_tile(lambda t: shift(t, 1), qs[pair[1]]))


def put_q3(qs, out_ref, indices):
    for p in indices:
        both = join(qs, PAIRS3[p])
        out_ref[pl.ds(p * K, K), :] = both[:, :C]
        out_ref[pl.ds(7 * K + 8 * p, 8), :] = pack_row(both[:, C:])


def ends3(q3_ref, p):
    return q3_ref[pl.ds(7 * K + 8 * p, 8), :]


def put_q2(qs, q3_ref, out_ref):
    both = join(qs, PAIRS2[0])
    out_ref[pl.ds(0, K), :] = both[:, :C]
    out_ref[pl.ds(K, 5 * K), :] = q3_ref[pl.ds(K, 5 * K), :]
    ends = [pack_row(both[:, C:])] + [ends3(q3_ref, p) for p in range(1, 6)]
    low = lanes((8, C)) % SLOT < H
    for j in range(3):
        both = jnp.where(low, shift(ends[j], -5), shift(ends[j + 3], 4))
        out_ref[pl.ds(6 * K + 8 * j, 8), :] = both


def put_q1(qs, q3_ref, out_ref):
    for p, core in enumerate((q3_ref[pl.ds(K, K), :], join(qs, (5, 10))[:, :C], q3_ref[pl.ds(5 * K, K), :])):
        out_ref[pl.ds(p * K, K), :] = core
    ends = [ends3(q3_ref, p) for p in range(1, 6)]
    at = lanes((8, C)) % SLOT
    both = shift(ends[3], 5)
    for k in (2, 1, 0):
        both = jnp.where(at < 4 * k + 4, shift(ends[k], 4 * k - 7), both)
    out_ref[pl.ds(3 * K, 8), :] = both
    out_ref[pl.ds(3 * K + 8, 8), :] = ends[4]
    inner = [pack_row(q3_ref[pl.ds(3 * K, K), :]), pack_row(join(qs, (6, 9))[:, :C])]
    out_ref[pl.ds(3 * K + 16, 8), :] = jnp.where(at < H, shift(inner[0], -5), shift(inner[1], 4))


def take_q1(in_ref, inner_ref, a):
    def put(pair, at, value):
        a[pair[0], :, at] = value
        a[pair[1], :, at] = shift(value, -1)

    core, side = pl.ds(0, C), pl.ds(C, C)
    for p, pair in enumerate(PAIRS1):
        packed = in_ref[pl.ds(3 * K + (8 if p == 4 else 0), 8), :]
        put(pair, side, unpack_row(packed if p == 4 else shift(packed, 7 - 4 * p)))
    for p, pair in enumerate(((3, 4), (5, 10), (11, 12))):
        put(pair, core, in_ref[pl.ds(p * K, K), :])
    lane = lanes((K, C))
    inside = (lane >= 4) & (lane < C - 4)
    packed = in_ref[pl.ds(3 * K + 16, 8), :]
    for pair, by in (((7, 8), 5), ((6, 9), -4)):
        ends = unpack_row(shift(packed, by))
        for i, value in zip(pair, (ends, shift(ends, -1))):
            a[i, :, core] = jnp.where(inside, inner_ref[i - 6], value)


def take_q(in_ref, pairs, write):
    for p, (first, second) in enumerate(pairs):
        n = len(pairs)
        ends = lambda j: in_ref[pl.ds(n * K + 8 * j, 8), :]
        packed = ends(p) if n == 7 else shift(ends(p % 3), 5 if p < 3 else -4)
        both = jnp.concatenate([in_ref[pl.ds(p * K, K), :], unpack_row(packed)], axis=1)
        write(first, both)
        write(second, by_tile(lambda t: shift(t, -1), both))


def put_ring(src, out_ref):
    for i, r in enumerate(RING):
        out_ref[pl.ds(Q1 + i * K, K), :] = src[H + r, :, :C]
    at = lanes((8, C)) % SLOT
    for i, r in enumerate(SIDE):
        a, b, c = (pack_row(src[H + r + d, :, :C]) for d in (0, 4, 8))
        both = jnp.where(at < 2 * REACH, shift(a, -2 * REACH), b)
        both = jnp.where(at < 4 * REACH, both, shift(c, 2 * REACH))
        out_ref[pl.ds(Q1 + len(RING) * K + 8 * i, 8), :] = both


def take_ring(in_ref, inner_ref):
    rows = {r: in_ref[pl.ds(Q1 + i * K, K), :] for i, r in enumerate(RING)}
    lane = lanes((K, C))
    inside = (lane >= REACH) & (lane < C - REACH)
    for i, r in enumerate(SIDE):
        packed = in_ref[pl.ds(Q1 + len(RING) * K + 8 * i, 8), :]
        for d, by in ((0, 2 * REACH), (4, 0), (8, -2 * REACH)):
            if r + d not in rows:
                ends = unpack_row(shift(packed, by))
                rows[r + d] = jnp.where(inside, inner_ref[pl.ds((r + d) * K, K), :], ends)
    return [rows[r] for r in range(R)]


def outer_rows(
    upper, slot_ref, mk_ref, side_ref, fine_mix, coarse_mix, halo_ref, states, cc_out, mk, cf, cc
):
    u0, u1, u2, u3, rs, gs, qs = states
    mk[...] = jnp.zeros_like(mk)
    first = 0 if upper else H + R
    for i, ends in enumerate(corner_ends(halo_ref, not upper)):
        u0[first + i, :, :C] = halo_ref[pl.ds(i * K, K), :]
        u0[first + i, :, C:] = jnp.zeros((K, C), jnp.float32) if ends is None else unpack_row(ends)
    at = H * K + 8 * HALF
    for j, ref, at, side, side_at in (
        (0 if upper else 2, halo_ref, at, halo_ref, at + 2 * R),
        (1, mk_ref, 0, side_ref, 8 * R),
    ):
        coefs = unpack_row(side[pl.ds(side_at, 8), :])
        for i in range(2):
            mk[2 * i, pl.ds(j * R, R), :] = ref[pl.ds(at + i * R, R), :]
            mk[2 * i + 1, pl.ds(j * R, R), :] = coefs[i * R : i * R + R]
    fine_coarse_coefficients(mk, R - 8, NC, cf, cc)
    mirror = lambda rows: rows if upper else [NC - 1 - i for i in rows]

    def rows_of(steps, wide, narrow, lowered):
        for margin, src, dst in ((1, u0, u1), (2, u1, u2), (3, u2, u3)):

            @pl.loop(*steps, unroll=steps[1] - steps[0])
            def _(i):
                r = margin + i if upper else E - 1 - margin - i
                dst[r] = step_row(src, r, cf, r + BASE, 1, fine_mix[...])

        for i in mirror(wide):
            rs[i] = restrict(u0, i, cc, i)
        for i in mirror(narrow):
            gs[i] = step_row(rs, i, cc, i, 2, coarse_mix[...])
        for i in mirror(lowered):
            fc = restrict(u3, i, cc, i)
            qs[i] = fc - gs[i] if narrow else fc

    for k in range(4):

        @pl.when(slot_ref[0] == float(k))
        def _():
            wide, narrow = ([*range(k - 1, 4)], [*range(k, 4)]) if k else ([], [])
            rows_of((2 * k, H), wide, [i + 1 for i in narrow], [*range(k + 1, 6)])

    half = pl.ds(0 if upper else NC // 2, NC // 2)
    for i in range(6):
        cc_out[i, half, :] = cc[i, half, :]


FIRST_UPPER = False


def first_side_kernel(*refs):
    *ins, mk, cf, cc = refs
    states, cc_out, q3_ref = ins[13:20], ins[20], ins[21]
    outer_rows(FIRST_UPPER, *ins[:6], states, cc_out, mk, cf, cc)

    @pl.when(ins[0][0] < 3.0)
    def _():
        put_q3(states[6], q3_ref, range(4) if FIRST_UPPER else range(3, 7))


def second_side_kernel(*refs):
    *ins, mk, cf, cc = refs
    states, cc_out, q3_ref, q2_ref = ins[15:22], ins[22], ins[23], ins[24]
    outer_rows(not FIRST_UPPER, *ins[:6], states, cc_out, mk, cf, cc)

    @pl.when(ins[0][0] < 3.0)
    def _():
        put_q3(states[6], q3_ref, range(4, 7) if FIRST_UPPER else range(3))
        put_q2(states[6], q3_ref, q2_ref)


def near_message_kernel(slot_ref, u3, qs, q3_ref, out_ref):
    @pl.when(slot_ref[0] < 3.0)
    def _():
        put_q1(qs, q3_ref, out_ref)
        put_ring(u3, out_ref)


def before_kernel(
    slot_ref, core_ref, fine_mix, coarse_mix, cf_ref, u3, cc_ref, mk_ref,
    inner_ref, rest_ref, qi_ref, ua, ub, rs, cc,
):
    for r in range(R):
        ua[r] = core_ref[pl.ds(r * K, K), :]
    for i in range(6):
        cc[i] = cc_ref[i, :, :C]
    for i in range(R // 2):
        rs[i] = block_mean((ua[2 * i], ua[2 * i + 1]), cc_ref, i)
    for margin, src, dst in ((1, ua, ub), (2, ub, ua), (3, ua, None)):
        for r in range(margin, R - margin):
            value = step_row(src, r, cf_ref, r, 1, fine_mix[...])
            if dst is None:
                inner_ref[pl.ds(r * K, K), :] = value
            else:
                dst[r] = value
    for r in RING:
        inner_ref[pl.ds(r * K, K), :] = jnp.zeros((K, C), jnp.float32)
    for i in range(2, 6):
        pair = [inner_ref[pl.ds(r * K, K), :] for r in (2 * i, 2 * i + 1)]
        g = step_row(rs, i, cc, 4 + i, 2, coarse_mix[...])
        qi_ref[i - 2] = block_mean(pair, cc_ref, i) - jnp.clip(slot_ref[0] - 1.0, 0.0, 1.0) * g
    for i in range(R // 2):
        pair = [u3[H + r, :, :C] for r in (2 * i, 2 * i + 1)]
        fc = spread(block_mean(pair, cc_ref, i))
        for r, value in zip((2 * i, 2 * i + 1), pair):
            rest_ref[pl.ds(r * K, K), :] = value - mk_ref[pl.ds(r, 1), :] * fc


def block_mean(pair, cc_ref, i):
    total = pair[0] + pair[1]
    return (total + shift(total, -1)) * cc_ref[5, 4 + i : 5 + i, :C]


def near_kernel(q1_ref, inner_ref, qi_ref, cc_ref, mk_ref, _, a, base_ref):
    take_q1(q1_ref, qi_ref, a)
    rows = take_ring(q1_ref, inner_ref)
    for i in range(R // 2):
        pair = rows[2 * i], rows[2 * i + 1]
        fc = spread(block_mean(pair, cc_ref, i))
        for r, value in zip((2 * i, 2 * i + 1), pair):
            base_ref[pl.ds(r * K, K), :] = value - mk_ref[pl.ds(r, 1), :] * fc


def far_kernel(coarse_mix, cc_ref, q3_ref, b, a):
    take_q(q3_ref, PAIRS3, lambda i, value: a.__setitem__(i, value))
    for i in range(2, 14):
        b[i] = step_row(a, i, cc_ref, i, 2, coarse_mix[...])


def last_kernel(
    slot_ref, mk_ref, coarse_mix, cc_ref, x_ref, far, near, q2_ref, qs, rest_ref, base_ref,
    out_hbm, next_hbm, a, b, out_ref, next_ref, sems,
):
    take_q(q2_ref, PAIRS2, lambda i, value: b.__setitem__(i, far[i] + value))
    for i in range(3, 13):
        a[i] = near[i] + step_row(b, i, cc_ref, i, 2, coarse_mix[...])
    first = slot_ref[0] == 0.0

    def put(ref, from_ref, i, value):
        value = spread(value)
        for r in (2 * i, 2 * i + 1):
            total = from_ref[pl.ds(r * K, K), :] + mk_ref[pl.ds(r, 1), :] * value
            ref[pl.ds(r, K, stride=R), :] = total

    @pl.when(first)
    def _():
        next_ref[...] = x_ref[...]

    @pl.when(jnp.logical_not(first))
    def _():
        for i in range(R // 2):
            put(next_ref, base_ref, i, a[4 + i, :, :C])

    next_copy = pltpu.make_async_copy(next_ref, next_hbm, sems.at[0])
    next_copy.start()
    halves = []
    for i in range(R // 2):
        z = qs[4 + i] + step_row(a, 4 + i, cc_ref, 4 + i, 2, coarse_mix[...])
        put(out_ref, rest_ref, i, z[:, :C])
        if i % 4 == 3:
            rows = pl.ds(i // 4 * 8, 8)
            halves.append(
                pltpu.make_async_copy(
                    out_ref.reshape(K, R, C).at[:, rows, :],
                    out_hbm.reshape(K, R, C).at[:, rows, :],
                    sems.at[1 + i // 4],
                )
            )
            halves[-1].start()
    for copy in (next_copy, *halves):
        copy.wait()


def f32(*shape):
    return jax.ShapeDtypeStruct(shape, jnp.float32)


def scratch(*shape):
    return pltpu.VMEM(shape, jnp.float32)


def call(kernel, n_in, outs, scratches=(), smem=0, aliases=None, out_spec=VMEM, cost=None):
    return pl.pallas_call(
        kernel,
        out_shape=outs,
        in_specs=[SMEM] * smem + [VMEM] * (n_in - smem),
        out_specs=jax.tree.map(lambda _: out_spec, outs),
        scratch_shapes=list(scratches),
        input_output_aliases=aliases or {},
        cost_estimate=cost,
        compiler_params=pltpu.CompilerParams(vmem_limit_bytes=40 * 1024 * 1024),
    )


def moved(value, axis, by, wrap=False):
    n = lax.axis_size(axis)
    pairs = [(i, (i + by) % n) for i in range(n) if wrap or 0 <= i + by < n]
    return lax.ppermute(value, axis, pairs)


def body(start, wet, kappa, mixing):
    x = start.reshape(K * R, C)
    slot = lax.axis_index("tm").astype(jnp.float32).reshape(1)
    mixing = mixing[None] * jnp.array([1.0, 3.0], jnp.float32)[:, None, None]
    lon = (R + 2) * 4
    left, right, core, mk = call(
        edge_kernel, 2, (f32(lon, C), f32(lon, C), f32(R * K, C), f32(2 * R, C))
    )(x, jnp.where(wet > 0, kappa, -kappa))
    from_left = moved(left, "lon", 1, True)
    from_right = moved(right, "lon", -1, True)
    matrix = jax.ShapeDtypeStruct((K, 3 * K), jnp.bfloat16)
    core, top, bottom, side, fine_mix, coarse_mix = call(
        halo_kernel,
        5,
        (f32(R * K, C), f32(LAT, C), f32(LAT, C), f32(8 * (R + 2), C), matrix, matrix),
        aliases={0: 0},
    )(core, mk, from_left, from_right, mixing)
    down = moved(top, "lat", -1)
    up = moved(bottom, "lat", 1)
    before = moved(core, "tm", 1)
    fine, coarse = f32(E, K, W), f32(NC, K, W)
    shapes = (fine,) * 4 + (coarse,) * 3
    *states, cf = call(
        own_kernel,
        6,
        shapes + (f32(5, R, C),),
        [scratch(4, R, C), scratch(5, R, W), scratch(6, R // 2, W)],
        smem=1,
    )(slot, core, side, mk, fine_mix, coarse_mix)
    parts = [scratch(4, 48, C), scratch(5, 48, W), scratch(6, NC, W)]
    coefs = f32(6, NC, W)
    states = call(
        first_side_kernel,
        13,
        shapes + (coefs, f32(Q3, C)),
        parts,
        smem=1,
        aliases={6 + i: i for i in range(7)},
    )(slot, mk, side, fine_mix, coarse_mix, up if FIRST_UPPER else down, *states)
    *states, cc, q3, q2 = call(
        second_side_kernel,
        15,
        shapes + (coefs, f32(Q3, C), f32(Q2, C)),
        parts,
        smem=1,
        aliases={6 + i: i for i in range(9)},
    )(slot, mk, side, fine_mix, coarse_mix, down if FIRST_UPPER else up, *states)
    u3, qs = states[3], states[6]
    q1 = call(
        near_message_kernel,
        4,
        f32(Q1 + RG, C),
        smem=1,
        cost=pl.CostEstimate(flops=300 * 10**8, bytes_accessed=0, transcendentals=0),
    )(slot, u3, qs, q3)
    q3, q2, q1 = moved(q3, "tm", 3), moved(q2, "tm", 2), moved(q1, "tm", 1)
    inner, rest, inner_q = call(
        before_kernel,
        8,
        (f32(R * K, C), f32(R * K, C), f32(4, K, C)),
        [scratch(R, K, C), scratch(R, K, C), scratch(R // 2, K, C), scratch(6, NC, C)],
        smem=1,
    )(slot, before, fine_mix, coarse_mix, cf, u3, cc, mk)
    far = call(
        far_kernel,
        3,
        coarse,
        [scratch(NC, K, W)],
        cost=pl.CostEstimate(flops=20 * 10**8, bytes_accessed=0, transcendentals=0),
    )(coarse_mix, cc, q3)
    near, base = call(near_kernel, 6, (coarse, f32(R * K, C)))(
        q1, inner, inner_q, cc, mk, far
    )
    out, following = call(
        last_kernel,
        11,
        (f32(K * R, C), f32(K * R, C)),
        [scratch(NC, K, W)] * 2 + [scratch(K * R, C)] * 2 + [pltpu.SemaphoreType.DMA((3,))],
        smem=1,
        out_spec=ANY,
    )(slot, mk, coarse_mix, cc, x, far, near, q2, qs, rest, base)
    return out.reshape(1, K, R, C), following.reshape(1, K, R, C)


def solution(mesh):
    in_specs = (P("tm", None, "lat", "lon"), P("lat", "lon"), P("lat", "lon"), P())
    out_specs = (P("tm", None, "lat", "lon"), P("tm", None, "lat", "lon"))
    return jax.shard_map(body, mesh=mesh, in_specs=in_specs, out_specs=out_specs, check_vma=False)
```
